32 devices in a mesh: groups: 2 (over y), loop: 4 (over z), enc: 2 (over x), rep: 2 (over core).
Axes of the slice: x: 2, y: 2, z: 4, core: 2. Of those that a mesh axis runs over, the one named last changes fastest.
Arguments:
- embeddings: bfloat16 [4096, 768], P(('groups', 'loop', 'rep'), 'enc'), parts along dimension 0, may hold values from -24 to 24
- head_weight: bfloat16 [768, 768], P('enc'), may hold values from -0.21875 to 0.21875
- gp_weights: float32 [4096], P('groups'), parts along dimension 0, may hold values from -24 to 24
- counts: int32 [8], P('groups'), parts along dimension 0, may hold values from 64 to 512, as said below
Outputs:
- embed_grad: bfloat16 [4096, 768], P(('groups', 'loop', 'rep'), 'enc'), parts along dimension 0
- head_grad: float32 [1536, 768], P(('groups', 'enc')), parts along dimension 0
The draws below stay inside these ranges and needn't reach their ends.
There are 2 independent parts, one for each index of `groups`. The reference program is written for one: setup_inputs(seed, part) draws one part's arguments, and reference() takes and returns one part's arrays. A program takes and returns all parts, laid end to end along the dimension named above; an argument that names none is the same for every part. Nothing has to cross between parts.
Inputs may be any that keep to these rules, and one draw needn't show every extreme that they name: `counts`: some block is full and some block holds exactly 64 valid molecules.
All inputs are finite; a program needn't handle non-finite values.
Results may differ from the reference program's by a relative error of at most 0.019.
Values may be sent and summed in bfloat16 or wider, within the bound.
No kernel may reach another device: no remote copies, remote signals or barrier semaphores. Data moves between devices by JAX's collectives and lax.ppermute only.
A program may use at most 64 MiB of HBM per device.

```python
import math
import jax
import jax.numpy as jnp
from jax import lax

E = 768
F = 768
BLOCK = 512
BLOCKS = 4
MOLS = 2048


def draw_embeddings(key, part):
    key = jax.random.fold_in(key, 11)
    key_base = jax.random.fold_in(key, 0)
    key_rows = jax.random.fold_in(key, 1)
    key_cols = jax.random.fold_in(key, 3)
    row_scale = jnp.exp(jax.random.uniform(key_rows, (MOLS, 1), jnp.float32, math.log(0.3), math.log(3.0)))
    col_scale = jnp.exp(jax.random.uniform(key_cols, (1, E), jnp.float32, math.log(0.5), math.log(2.0)))
    base = jax.random.normal(key_base, (MOLS, E), jnp.float32)
    base = jnp.clip(base, -4.0, 4.0)
    return (base * row_scale * col_scale).astype(jnp.bfloat16)


def draw_counts(key, part):
    key = jax.random.fold_in(key, 7)
    key_draw, key_full, key_low = jax.random.split(key, 3)
    values = jax.random.randint(key_draw, (BLOCKS,), BLOCK // 8, BLOCK + 1)
    full_at = jax.random.randint(key_full, (), 0, BLOCKS)
    low_at = (full_at + 1 + jax.random.randint(key_low, (), 0, BLOCKS - 1)) % BLOCKS
    values = values.at[full_at].set(BLOCK).at[low_at].set(BLOCK // 8)
    return values.astype(jnp.int32)


def level_of(stream_key, dims, pieces, low, top_value):
    factor_of = 1.0
    for dim, shards_of in pieces:
        steps = jax.random.uniform(jax.random.fold_in(jax.random.fold_in(stream_key, 6), dim), (shards_of,), jnp.float32, low / len(pieces), top_value / len(pieces))
        factor_of = factor_of * jnp.repeat(jnp.exp(steps), dims[dim] // shards_of).reshape((-1,) + (1,) * (len(dims) - 1 - dim))
    return factor_of


def centred(key, shape, width, reach, pieces=(), kind=jnp.bfloat16):
    loudness = level_of(key, shape, pieces, -0.22, 0.18) if pieces else 1.0
    drawn = jax.random.normal(key, shape, jnp.float32) * width * loudness
    return jnp.minimum(jnp.maximum(drawn, -reach), reach).astype(kind)


def setup_inputs(seed: int = 0, part: int = 0) -> dict:
    streams_of = jax.random.split(jax.random.key(seed), 5)
    part_keys = jax.random.split(jax.random.fold_in(streams_of[4], part), 5)
    embeddings = draw_embeddings(jax.random.fold_in(jax.random.fold_in(streams_of[4], part), 71), part)
    head_weight = centred(streams_of[1], (E, F), E ** -0.5, 0.21875, ((0, 2),))
    gp_weights = centred(part_keys[2], (MOLS,), 4.0, 24.0, (), jnp.float32)
    counts = draw_counts(jax.random.fold_in(jax.random.fold_in(streams_of[4], part), 71), part)
    return {"embeddings": embeddings, "head_weight": head_weight, "gp_weights": gp_weights, "counts": counts}


EPSILON = 1e-6


def reference(embeddings, head_weight, gp_weights, counts):
    features = jnp.dot(embeddings, head_weight, preferred_element_type=jnp.float32).astype(jnp.bfloat16)
    wide = features.astype(jnp.float32)
    norms = jnp.sum(wide * wide, axis=1)
    total = embeddings.shape[0]
    rows_all = jnp.arange(total, dtype=jnp.int32)
    block_of = rows_all // BLOCK
    inside = rows_all % BLOCK
    limit = counts[block_of]
    weights = jnp.where(inside < limit, gp_weights, jnp.zeros_like(gp_weights))

    def one_block(block_index):
        start = (block_index * BLOCK).astype(jnp.int32)
        left = lax.dynamic_slice_in_dim(features, start, BLOCK, 0)
        left_norms = lax.dynamic_slice_in_dim(norms, start, BLOCK, 0)
        left_weights = lax.dynamic_slice_in_dim(weights, start, BLOCK, 0)
        scores = jnp.dot(left, features.T, preferred_element_type=jnp.float32)
        denom = left_norms[:, None] + norms[None, :] - scores + EPSILON
        inverse = 1.0 / (denom * denom)
        pair_coef = left_weights[:, None] * weights[None, :]
        pair_weight = (pair_coef * (left_norms[:, None] + norms[None, :]) * inverse).astype(jnp.bfloat16)
        quotient = jnp.sum(pair_coef * 2.0 * scores * inverse, axis=1)
        carried = jnp.dot(pair_weight, features, preferred_element_type=jnp.float32)
        return carried - left.astype(jnp.float32) * quotient[:, None]

    grads = lax.map(one_block, jnp.arange(total // BLOCK, dtype=jnp.int32))
    grad_features = grads.reshape(total, features.shape[1])
    feature_grad = grad_features.astype(jnp.bfloat16)
    embed_grad = jnp.dot(feature_grad, head_weight.T, preferred_element_type=jnp.float32).astype(jnp.bfloat16)
    head_grad = jnp.dot(embeddings.T, feature_grad, preferred_element_type=jnp.float32)
    return embed_grad, head_grad
```

```python
import jax
import jax.numpy as jnp
from jax import lax
from jax.experimental import pallas as pl
from jax.experimental.pallas import tpu as pltpu
from jax.sharding import PartitionSpec as P

EPSILON = 1e-06
TILE = 128
CHUNK = 2 * TILE


def passed_along(value, axis, steps):
    count = lax.axis_size(axis)
    pairs = [(source, (source + steps) % count) for source in range(count)]
    return lax.ppermute(value, axis, pairs)


def ring_body(embeddings, head_weight, gp_weights, counts):
    enc_size = lax.axis_size("enc")
    rep_size = lax.axis_size("rep")
    loop_size = lax.axis_size("loop")
    share_rows = embeddings.shape[0]
    piece_rows = share_rows // enc_size
    block_rows = share_rows * rep_size
    loop_index = lax.axis_index("loop")
    enc_index = lax.axis_index("enc")
    rep_index = lax.axis_index("rep")
    own_feats = lax.psum_scatter(
        jnp.dot(embeddings, head_weight, preferred_element_type=jnp.float32),
        "enc",
        scatter_dimension=0,
        tiled=True,
    ).astype(jnp.bfloat16)
    block_feats = lax.all_gather(own_feats, ("enc", "rep"), axis=0, tiled=True)
    block_norms = jnp.sum(jnp.square(block_feats.astype(jnp.float32)), axis=1)
    offsets = (
        jnp.arange(rep_size, dtype=jnp.int32)[None, :, None] * share_rows
        + jnp.arange(enc_size, dtype=jnp.int32)[:, None, None] * piece_rows
        + jnp.arange(piece_rows, dtype=jnp.int32)[None, None, :]
    ).reshape(block_rows)
    own_base = lax.dynamic_slice_in_dim(gp_weights, loop_index * block_rows, block_rows)
    block_coef = (
        own_base.reshape(rep_size, enc_size, piece_rows).transpose(1, 0, 2).reshape(block_rows)
    )
    own_count = lax.dynamic_index_in_dim(counts, loop_index, keepdims=False)
    block_coef = jnp.where(offsets < own_count, block_coef, 0.0)
    piece_start = rep_index * share_rows + enc_index * piece_rows
    piece_offsets = piece_start + jnp.arange(piece_rows, dtype=jnp.int32)

    def tile(state, piece, anchor):
        anchor_count = lax.dynamic_index_in_dim(counts, anchor, keepdims=False)
        accum, quotient_sum = state
        piece_coef = lax.dynamic_slice_in_dim(
            gp_weights, anchor * block_rows + piece_start, piece_rows
        )
        piece_coef = jnp.where(piece_offsets < anchor_count, piece_coef, 0.0)
        piece_norms = jnp.sum(jnp.square(piece.astype(jnp.float32)), axis=1)
        scores = lax.dot_general(
            piece, block_feats, (((1,), (1,)), ((), ())), preferred_element_type=jnp.float32
        )
        denom = piece_norms[:, None] + block_norms[None, :] - scores + EPSILON
        inverse = 1.0 / (denom * denom)
        pair_coef = piece_coef[:, None] * block_coef[None, :]
        pair_weight = (pair_coef * (piece_norms[:, None] + block_norms[None, :]) * inverse).astype(
            jnp.bfloat16
        )
        quotient_sum = quotient_sum + jnp.sum(pair_coef * 2.0 * scores * inverse, axis=0)
        accum = accum + lax.dot_general(
            pair_weight, piece, (((0,), (0,)), ((), ())), preferred_element_type=jnp.float32
        )
        return (accum, quotient_sum)

    start_state = (
        jnp.zeros((block_rows, block_feats.shape[1]), jnp.float32),
        jnp.zeros((block_rows,), jnp.float32),
    )
    state = tile(start_state, own_feats, loop_index)

    def forward_step(step_index, carry):
        moving, inner = carry
        moving = passed_along(moving, "loop", 1)
        inner = tile(inner, moving, (loop_index - step_index - 1 + loop_size) % loop_size)
        return (moving, inner)

    moving, state = lax.fori_loop(0, loop_size - 1, forward_step, (own_feats, state))
    accum, quotient_sum = state
    grad_block = accum - block_feats.astype(jnp.float32) * quotient_sum[:, None]
    own_grad = lax.psum_scatter(
        grad_block.astype(jnp.bfloat16), ("enc", "rep"), scatter_dimension=0, tiled=True
    )
    piece = lax.all_gather(own_grad, "enc", axis=0, tiled=True)
    embed_part = lax.dot_general(
        piece, head_weight, (((1,), (1,)), ((), ())), preferred_element_type=jnp.float32
    )
    head_part = lax.dot_general(
        embeddings, piece, (((0,), (0,)), ((), ())), preferred_element_type=jnp.float32
    )
    head_grad = lax.psum(head_part, ("loop", "rep"))
    return (embed_part.astype(jnp.bfloat16), head_grad)


def turned(row):
    return jnp.transpose(jnp.broadcast_to(row, (TILE, TILE)))[:, :1]


def group_kernel(loop_size, *refs):
    n_pieces = 2 * loop_size
    counts_ref, gp_ref = refs[0], refs[1]
    head_ref = refs[2]
    far_head_refs = refs[3:5]
    near_refs = refs[5 : 5 + n_pieces]
    far_refs = refs[5 + n_pieces : 5 + 2 * n_pieces]
    embed_out, head_out = refs[5 + 2 * n_pieces : 7 + 2 * n_pieces]
    near, far, far_head, feats, weights, norm_rows, accum, quotient, grads, sems, head_sems = refs[
        7 + 2 * n_pieces :
    ]
    piece_rows = near_refs[0].shape[0]
    halves = piece_rows // TILE
    block_rows = 2 * piece_rows
    z = lax.axis_index("loop")
    rep = lax.axis_index("rep")
    enc_rows, width = head_ref.shape
    half_rows = enc_rows // 2

    head_copies = [
        pltpu.make_async_copy(
            far_head_refs[0], far_head.at[pl.ds(rep * half_rows, half_rows)], head_sems.at[0]
        ),
        pltpu.make_async_copy(
            far_head_refs[1], far_head.at[pl.ds((1 - rep) * half_rows, half_rows)], head_sems.at[1]
        ),
    ]
    for copy in head_copies:
        copy.start()

    total = jnp.int32(0)
    own_start = jnp.int32(0)
    copies = []
    lane = lax.broadcasted_iota(jnp.int32, (1, TILE), 1)
    for r in range(2):
        for k in range(loop_size):
            block = jnp.bitwise_xor(z, k)
            count = counts_ref[block]
            if k == 0:
                own_start = jnp.where(rep == r, total, own_start)
            for h in range(halves):
                base = r * piece_rows + h * TILE
                valid = count > base
                at = pl.multiple_of(total * TILE, TILE)
                slot = (r * loop_size + k) * halves + h
                for side, (source, target) in enumerate(((near_refs, near), (far_refs, far))):
                    for who in range(2):
                        copy = pltpu.make_async_copy(
                            source[who * loop_size + k].at[pl.ds(h * TILE, TILE)],
                            target.at[pl.ds(at, TILE)],
                            sems.at[side * n_pieces * halves + slot],
                        )
                        mine = rep == (r if who == 0 else 1 - r)
                        copies.append((jnp.logical_and(valid, mine), copy))

                @pl.when(valid)
                def _(block=block, base=base, count=count, total=total):
                    row = gp_ref[pl.ds(block * (block_rows // TILE) + base // TILE, 1), :]
                    weights[pl.ds(total, 1), :] = jnp.where(lane + base < count, row, 0.0)

                total = total + valid.astype(jnp.int32)
    for wanted, copy in copies:
        pl.when(wanted)(copy.start)
    tail = pl.multiple_of(total * TILE, TILE)
    near[pl.ds(tail, TILE), :] = jnp.zeros((TILE, enc_rows), jnp.bfloat16)
    far[pl.ds(tail, TILE), :] = jnp.zeros((TILE, enc_rows), jnp.bfloat16)
    feats[pl.ds(tail, TILE), :] = jnp.zeros((TILE, width), jnp.bfloat16)
    weights[pl.ds(total, 1), :] = jnp.zeros((1, TILE), jnp.float32)
    for copy in head_copies:
        copy.wait()
    for wanted, copy in copies:
        pl.when(wanted)(copy.wait)

    chunks = (total + 1) // 2

    def features(c, _):
        rows = pl.ds(pl.multiple_of(c * CHUNK, CHUNK), CHUNK)
        value = jnp.dot(near[rows, :], head_ref[...], preferred_element_type=jnp.float32)
        value += jnp.dot(far[rows, :], far_head[...], preferred_element_type=jnp.float32)
        value = value.astype(jnp.bfloat16)
        feats[rows, :] = value
        wide = value.astype(jnp.float32)
        square = wide * wide
        part = square[:, :TILE]
        for s in range(1, width // TILE):
            part += square[:, s * TILE : (s + 1) * TILE]
        norm_rows[pl.ds(c, 1), :] = jnp.sum(jnp.transpose(part), axis=0, keepdims=True)
        return 0

    lax.fori_loop(0, chunks, features, 0)

    half = (total + 1) // 2
    first = jnp.where(rep == 0, 0, half)
    last = jnp.where(rep == 0, half, total)
    head_out[...] = jnp.zeros_like(head_out)

    def row_chunk(i, _):
        tile = first + 2 * i
        rows = pl.ds(pl.multiple_of(tile * TILE, TILE), CHUNK)
        left = feats[rows, :]
        left_wide = left.astype(jnp.float32)
        left_norms = jnp.sum(left_wide * left_wide, axis=1, keepdims=True)
        accum[...] = jnp.zeros_like(accum)
        quotient[...] = jnp.zeros_like(quotient)

        def col_chunk(c, _):
            cols = pl.ds(pl.multiple_of(c * CHUNK, CHUNK), CHUNK)
            right = feats[cols, :]
            scores = lax.dot_general(
                left, right, (((1,), (1,)), ((), ())), preferred_element_type=jnp.float32
            )
            both = left_norms + norm_rows[pl.ds(c, 1), :]
            denom = both - scores + EPSILON
            coef = jnp.concatenate(
                [weights[pl.ds(2 * c, 1), :], weights[pl.ds(2 * c + 1, 1), :]], axis=1
            )
            scaled = coef * (1.0 / (denom * denom))
            pair = (scaled * both).astype(jnp.bfloat16)
            terms = scaled * scores
            quotient[...] += terms[:, :TILE] + terms[:, TILE:]
            accum[...] += jnp.dot(pair, right, preferred_element_type=jnp.float32)
            return 0

        lax.fori_loop(0, chunks, col_chunk, 0)
        quot = 2.0 * jnp.sum(quotient[...], axis=1, keepdims=True)
        coef = jnp.concatenate(
            [turned(weights[pl.ds(tile, 1), :]), turned(weights[pl.ds(tile + 1, 1), :])], axis=0
        )
        row = lax.broadcasted_iota(jnp.int32, (CHUNK, 1), 0)
        coef = jnp.where(row < (last - tile) * TILE, coef, 0.0)
        grad = (coef * (accum[...] - left_wide * quot)).astype(jnp.bfloat16)
        grads[rows, :] = grad
        head_out[...] += lax.dot_general(
            near[rows, :], grad, (((0,), (0,)), ((), ())), preferred_element_type=jnp.float32
        )
        return 0

    lax.fori_loop(0, (last - first + 1) // 2, row_chunk, 0)

    own_valid = counts_ref[z] - rep * piece_rows
    own = grads[pl.ds(pl.multiple_of(own_start * TILE, TILE), piece_rows), :]
    row = lax.broadcasted_iota(jnp.int32, (piece_rows, 1), 0)
    own = jnp.where(row < own_valid, own, jnp.zeros_like(own))
    embed_out[...] = lax.dot_general(
        own, head_ref[...], (((1,), (1,)), ((), ())), preferred_element_type=jnp.float32
    ).astype(embed_out.dtype)


def gathered_body(embeddings, head_weight, gp_weights, counts):
    loop_size = lax.axis_size("loop")
    rep = lax.axis_index("rep")
    share_rows, share_cols = embeddings.shape
    enc_rows, width = head_weight.shape

    def across_z(value, step):
        return lax.ppermute(value, "loop", [(i, i ^ step) for i in range(loop_size)])

    def across_x(value):
        return lax.ppermute(value, "enc", [(0, 1), (1, 0)])

    def across_cores(value):
        return lax.ppermute(value, "rep", [(0, 1), (1, 0)])

    head_half = lax.dynamic_slice_in_dim(head_weight, rep * (enc_rows // 2), enc_rows // 2, 0)
    near3 = across_z(embeddings, 3)
    near1 = across_z(embeddings, 1)
    far0 = across_x(embeddings)
    far_head = across_x(head_half)
    near2 = across_z(near3, 1)
    far2 = across_z(far0, 2)
    far1 = across_x(near1)
    far3 = across_x(near3)
    near = [embeddings, near1, near2, near3]
    far = [far0, far1, far2, far3]
    near_other = [across_cores(value) for value in near]
    far_other = [across_cores(value) for value in far]
    head_other = across_cores(far_head)

    molecules = gp_weights.shape[0]
    n_pieces = 2 * loop_size
    tiles = molecules // TILE
    anywhere = pl.BlockSpec(memory_space=pl.ANY)
    vmem = pl.BlockSpec(memory_space=pltpu.VMEM)
    embed_grad, head_part = pl.pallas_call(
        lambda *refs: group_kernel(loop_size, *refs),
        out_shape=(
            jax.ShapeDtypeStruct((share_rows, share_cols), jnp.bfloat16),
            jax.ShapeDtypeStruct((enc_rows, width), jnp.float32),
        ),
        in_specs=[pl.BlockSpec(memory_space=pltpu.SMEM), vmem, vmem]
        + [anywhere] * (2 + 2 * n_pieces),
        out_specs=(vmem, vmem),
        scratch_shapes=[
            pltpu.VMEM((molecules + TILE, share_cols), jnp.bfloat16),
            pltpu.VMEM((molecules + TILE, share_cols), jnp.bfloat16),
            pltpu.VMEM((enc_rows, width), jnp.bfloat16),
            pltpu.VMEM((molecules + CHUNK, width), jnp.bfloat16),
            pltpu.VMEM((tiles + 8, TILE), jnp.float32),
            pltpu.VMEM((tiles // 2 + 8, CHUNK), jnp.float32),
            pltpu.VMEM((CHUNK, width), jnp.float32),
            pltpu.VMEM((CHUNK, TILE), jnp.float32),
            pltpu.VMEM((molecules + CHUNK, width), jnp.bfloat16),
            pltpu.SemaphoreType.DMA((2 * tiles,)),
            pltpu.SemaphoreType.DMA((2,)),
        ],
        compiler_params=pltpu.CompilerParams(vmem_limit_bytes=40 * 2**20),
    )(
        counts,
        gp_weights.reshape(tiles, TILE),
        head_weight,
        far_head,
        head_other,
        *near,
        *near_other,
        *far,
        *far_other,
    )
    head_grad = head_part + across_cores(head_part)
    return embed_grad, head_grad


def solution(mesh):
    placed = (P(("groups", "loop", "rep"), "enc"), P("enc", None), P("groups"), P("groups"))
    sizes = dict(mesh.shape)

    def body(*arrays):
        share_rows = arrays[0].shape[0]
        small = sizes["loop"] == 4 and sizes["enc"] == 2 and sizes["rep"] == 2
        if small and share_rows % CHUNK == 0:
            return gathered_body(*arrays)
        return ring_body(*arrays)

    return jax.shard_map(
        body,
        mesh=mesh,
        in_specs=placed,
        out_specs=(P(("groups", "loop", "rep"), "enc"), P(("groups", "enc"), None)),
        check_vma=False,
    )
```

```python
import jax
import jax.numpy as jnp
from jax import lax
from jax.experimental import pallas as pl
from jax.experimental.pallas import tpu as pltpu
from jax.sharding import PartitionSpec as P

EPSILON = 1e-06
TILE = 128
CHUNK = 2 * TILE


def passed_along(value, axis, steps):
    count = lax.axis_size(axis)
    pairs = [(source, (source + steps) % count) for source in range(count)]
    return lax.ppermute(value, axis, pairs)


def ring_body(embeddings, head_weight, gp_weights, counts):
    enc_size = lax.axis_size("enc")
    rep_size = lax.axis_size("rep")
    loop_size = lax.axis_size("loop")
    share_rows = embeddings.shape[0]
    piece_rows = share_rows // enc_size
    block_rows = share_rows * rep_size
    loop_index = lax.axis_index("loop")
    enc_index = lax.axis_index("enc")
    rep_index = lax.axis_index("rep")
    own_feats = lax.psum_scatter(
        jnp.dot(embeddings, head_weight, preferred_element_type=jnp.float32),
        "enc",
        scatter_dimension=0,
        tiled=True,
    ).astype(jnp.bfloat16)
    block_feats = lax.all_gather(own_feats, ("enc", "rep"), axis=0, tiled=True)
    block_norms = jnp.sum(jnp.square(block_feats.astype(jnp.float32)), axis=1)
    offsets = (
        jnp.arange(rep_size, dtype=jnp.int32)[None, :, None] * share_rows
        + jnp.arange(enc_size, dtype=jnp.int32)[:, None, None] * piece_rows
        + jnp.arange(piece_rows, dtype=jnp.int32)[None, None, :]
    ).reshape(block_rows)
    own_base = lax.dynamic_slice_in_dim(gp_weights, loop_index * block_rows, block_rows)
    block_coef = (
        own_base.reshape(rep_size, enc_size, piece_rows).transpose(1, 0, 2).reshape(block_rows)
    )
    own_count = lax.dynamic_index_in_dim(counts, loop_index, keepdims=False)
    block_coef = jnp.where(offsets < own_count, block_coef, 0.0)
    piece_start = rep_index * share_rows + enc_index * piece_rows
    piece_offsets = piece_start + jnp.arange(piece_rows, dtype=jnp.int32)

    def tile(state, piece, anchor):
        anchor_count = lax.dynamic_index_in_dim(counts, anchor, keepdims=False)
        accum, quotient_sum = state
        piece_coef = lax.dynamic_slice_in_dim(
            gp_weights, anchor * block_rows + piece_start, piece_rows
        )
        piece_coef = jnp.where(piece_offsets < anchor_count, piece_coef, 0.0)
        piece_norms = jnp.sum(jnp.square(piece.astype(jnp.float32)), axis=1)
        scores = lax.dot_general(
            piece, block_feats, (((1,), (1,)), ((), ())), preferred_element_type=jnp.float32
        )
        denom = piece_norms[:, None] + block_norms[None, :] - scores + EPSILON
        inverse = 1.0 / (denom * denom)
        pair_coef = piece_coef[:, None] * block_coef[None, :]
        pair_weight = (pair_coef * (piece_norms[:, None] + block_norms[None, :]) * inverse).astype(
            jnp.bfloat16
        )
        quotient_sum = quotient_sum + jnp.sum(pair_coef * 2.0 * scores * inverse, axis=0)
        accum = accum + lax.dot_general(
            pair_weight, piece, (((0,), (0,)), ((), ())), preferred_element_type=jnp.float32
        )
        return (accum, quotient_sum)

    start_state = (
        jnp.zeros((block_rows, block_feats.shape[1]), jnp.float32),
        jnp.zeros((block_rows,), jnp.float32),
    )
    state = tile(start_state, own_feats, loop_index)

    def forward_step(step_index, carry):
        moving, inner = carry
        moving = passed_along(moving, "loop", 1)
        inner = tile(inner, moving, (loop_index - step_index - 1 + loop_size) % loop_size)
        return (moving, inner)

    moving, state = lax.fori_loop(0, loop_size - 1, forward_step, (own_feats, state))
    accum, quotient_sum = state
    grad_block = accum - block_feats.astype(jnp.float32) * quotient_sum[:, None]
    own_grad = lax.psum_scatter(
        grad_block.astype(jnp.bfloat16), ("enc", "rep"), scatter_dimension=0, tiled=True
    )
    piece = lax.all_gather(own_grad, "enc", axis=0, tiled=True)
    embed_part = lax.dot_general(
        piece, head_weight, (((1,), (1,)), ((), ())), preferred_element_type=jnp.float32
    )
    head_part = lax.dot_general(
        embeddings, piece, (((0,), (0,)), ((), ())), preferred_element_type=jnp.float32
    )
    head_grad = lax.psum(head_part, ("loop", "rep"))
    return (embed_part.astype(jnp.bfloat16), head_grad)


OWN_ORDER = ((0, 0), (0, 1), (2, 0), (2, 1), (3, 1), (3, 0), (1, 1), (1, 0))
SLOTS = [(0, k, h) for k, h in OWN_ORDER] + [(1, k, h) for k, h in OWN_ORDER[::-1]]
LENT = ((1, 0), (1, 1), (3, 0), (3, 1))
PLACES = 24


def turned(row):
    return jnp.transpose(jnp.broadcast_to(row, (TILE, TILE)))[:, :1]


def prep_kernel(counts_ref, gp_ref, weights, places):
    z = lax.axis_index("loop")
    rep = lax.axis_index("rep")
    lane = lax.broadcasted_iota(jnp.int32, (1, TILE), 1)
    weights[...] = jnp.zeros_like(weights)
    total = jnp.int32(0)
    totals = []
    for slot, (other, k, h) in enumerate(SLOTS):
        block = jnp.bitwise_xor(z, k)
        piece = rep if other == 0 else 1 - rep
        base = piece * (2 * TILE) + h * TILE
        count = counts_ref[block]
        valid = count > base

        @pl.when(valid)
        def _(block=block, piece=piece, h=h, base=base, count=count, total=total):
            row = gp_ref[pl.ds(block * 4 + piece * 2 + h, 1), :]
            weights[pl.ds(total, 1), :] = jnp.where(lane + base < count, row, 0.0)

        places[slot] = jnp.where(valid, total, -1)
        total = total + valid.astype(jnp.int32)
        totals.append(total)
    own = totals[len(OWN_ORDER) - 1]
    places[16] = total
    places[17] = jnp.where(rep == 0, (total + 1) // 2, total // 2)
    places[18] = jnp.clip(counts_ref[z] - rep * (2 * TILE), 0, 2 * TILE)
    places[19] = own


def pair_kernel(places, weights, head_ref, *refs):
    near_refs, lent_refs = refs[:4], {1: refs[4], 3: refs[5]}
    feat_refs = (refs[6:10], refs[10:14])
    embed_out, head_out = refs[14:16]
    near, feats, norms, grads = refs[16:]
    width = head_ref.shape[1]
    total, rows_here, own_valid = places[16], places[17], places[18]

    def tile_at(place):
        return pl.ds(pl.multiple_of(place * TILE, TILE), TILE)

    for slot, (other, k, h) in enumerate(SLOTS):
        place = places[slot]

        @pl.when(place >= 0)
        def _(place=place, other=other, k=k, h=h):
            here = slice(h * TILE, (h + 1) * TILE)
            value = feat_refs[other][k][here, :]
            feats[tile_at(place), :] = value
            wide = value.astype(jnp.float32)
            square = wide * wide
            part = square[:, :TILE]
            for s in range(1, width // TILE):
                part += square[:, s * TILE : (s + 1) * TILE]
            norms[pl.ds(place, 1), :] = jnp.sum(jnp.transpose(part), axis=0, keepdims=True)
            if other == 0:
                near[tile_at(place), :] = near_refs[k][here, :]
            elif (k, h) in LENT:
                near[tile_at(place), :] = lent_refs[k][here, :]

    feats[tile_at(total), :] = jnp.zeros((TILE, width), jnp.bfloat16)
    norms[pl.ds(total, 1), :] = jnp.zeros((1, TILE), jnp.float32)

    def row_chunk(i, tiles):
        rows = pl.ds(pl.multiple_of(i * CHUNK, CHUNK), CHUNK)
        left = feats[rows, :]
        right = feats[: tiles * TILE, :]
        pair_of = [pl.ds(2 * i, 1), pl.ds(2 * i + 1, 1)]
        left_norms = jnp.concatenate([turned(norms[at, :]) for at in pair_of], axis=0)
        coef = jnp.concatenate([turned(weights[at, :]) for at in pair_of], axis=0)
        scores = lax.dot_general(
            left, right, (((1,), (1,)), ((), ())), preferred_element_type=jnp.float32
        )
        all_norms = jnp.concatenate([norms[t : t + 1, :] for t in range(tiles)], axis=1)
        all_coef = jnp.concatenate([weights[t : t + 1, :] for t in range(tiles)], axis=1)
        both = left_norms + all_norms
        denom = both - scores + EPSILON
        scaled = all_coef * (1.0 / (denom * denom))
        pair = (scaled * both).astype(jnp.bfloat16)
        quotient = 2.0 * jnp.sum(scaled * scores, axis=1, keepdims=True)
        carried = jnp.dot(pair, right, preferred_element_type=jnp.float32)
        row = lax.broadcasted_iota(jnp.int32, (CHUNK, 1), 0) + i * CHUNK
        coef = jnp.where(row < rows_here * TILE, coef, 0.0)
        grad = coef * (carried - left.astype(jnp.float32) * quotient)
        grads[rows, :] = grad.astype(jnp.bfloat16)

    chunks = (rows_here + 1) // 2
    behind = 2 * chunks - 1

    @pl.when(behind >= rows_here)
    def _():
        near[tile_at(behind), :] = jnp.zeros((TILE, near.shape[1]), near.dtype)

    col_tiles = jnp.maximum(2 * ((total + 1) // 2), 8)
    for tiles in (8, 10, 12, 14):

        @pl.when(col_tiles == tiles)
        def _(tiles=tiles):
            def step(i, _):
                row_chunk(i, tiles)
                return 0

            lax.fori_loop(0, chunks, step, 0)

    for count in (1, 2, 3, 4):

        @pl.when(chunks == count)
        def _(count=count):
            rows = slice(0, count * CHUNK)
            head_out[...] = lax.dot_general(
                near[rows, :],
                grads[rows, :],
                (((0,), (0,)), ((), ())),
                preferred_element_type=jnp.float32,
            )

    own = grads[:CHUNK, :]
    row = lax.broadcasted_iota(jnp.int32, (CHUNK, 1), 0)
    own = jnp.where(row < own_valid, own, jnp.zeros_like(own))
    embed_out[...] = lax.dot_general(
        own, head_ref[...], (((1,), (1,)), ((), ())), preferred_element_type=jnp.float32
    ).astype(embed_out.dtype)


def gathered_body(embeddings, head_weight, gp_weights, counts):
    loop_size = lax.axis_size("loop")
    rep = lax.axis_index("rep")
    share_rows, share_cols = embeddings.shape
    enc_rows, width = head_weight.shape

    def across_z(value, step):
        return lax.ppermute(value, "loop", [(i, i ^ step) for i in range(loop_size)])

    def across_x(value):
        return lax.ppermute(value, "enc", [(0, 1), (1, 0)])

    def across_cores(value):
        return lax.ppermute(value, "rep", [(0, 1), (1, 0)])

    smem = pl.BlockSpec(memory_space=pltpu.SMEM)
    vmem = pl.BlockSpec(memory_space=pltpu.VMEM)
    weights, places = pl.pallas_call(
        prep_kernel,
        out_shape=(
            jax.ShapeDtypeStruct((PLACES, TILE), jnp.float32),
            jax.ShapeDtypeStruct((PLACES,), jnp.int32),
        ),
        in_specs=[smem, vmem],
        out_specs=(vmem, smem),
    )(counts, gp_weights.reshape(-1, TILE))

    far0 = across_x(embeddings)
    near3 = across_z(embeddings, 3)
    near1 = across_z(embeddings, 1)
    half = enc_rows // 2
    head_mine = across_x(lax.dynamic_slice_in_dim(head_weight, rep * half, half, 0))
    head_other = across_cores(head_mine)
    far_head = jnp.where(
        rep == 0,
        jnp.concatenate([head_mine, head_other]),
        jnp.concatenate([head_other, head_mine]),
    )
    near2 = across_z(near3, 1)
    far2 = across_z(far0, 2)
    far1 = across_x(near1)
    far3 = across_x(near3)
    near = [embeddings, near1, near2, near3]
    far = [far0, far1, far2, far3]
    feats = [
        (
            jnp.dot(a, head_weight, preferred_element_type=jnp.float32)
            + jnp.dot(b, far_head, preferred_element_type=jnp.float32)
        ).astype(jnp.bfloat16)
        for a, b in zip(near, far)
    ]
    feats_other = [across_cores(value) for value in feats]
    lent = [across_cores(near1), across_cores(near3)]

    embed_grad, head_part = pl.pallas_call(
        pair_kernel,
        out_shape=(
            jax.ShapeDtypeStruct((share_rows, share_cols), jnp.bfloat16),
            jax.ShapeDtypeStruct((enc_rows, width), jnp.float32),
        ),
        in_specs=[smem] + [vmem] * 16,
        out_specs=(vmem, vmem),
        scratch_shapes=[
            pltpu.VMEM((12 * TILE, share_cols), jnp.bfloat16),
            pltpu.VMEM((18 * TILE, width), jnp.bfloat16),
            pltpu.VMEM((PLACES, TILE), jnp.float32),
            pltpu.VMEM((4 * CHUNK, width), jnp.bfloat16),
        ],
        compiler_params=pltpu.CompilerParams(vmem_limit_bytes=40 * 2**20),
    )(places, weights, head_weight, *near, *lent, *feats, *feats_other)
    head_grad = head_part + across_cores(head_part)
    return embed_grad, head_grad


def solution(mesh):
    placed = (P(("groups", "loop", "rep"), "enc"), P("enc", None), P("groups"), P("groups"))
    sizes = dict(mesh.shape)

    def body(*arrays):
        share_rows = arrays[0].shape[0]
        small = sizes["loop"] == 4 and sizes["enc"] == 2 and sizes["rep"] == 2
        if small and share_rows == 2 * TILE:
            return gathered_body(*arrays)
        return ring_body(*arrays)

    return jax.shard_map(
        body,
        mesh=mesh,
        in_specs=placed,
        out_specs=(P(("groups", "loop", "rep"), "enc"), P(("groups", "enc"), None)),
        check_vma=False,
    )
```

```python
import jax
import jax.numpy as jnp
from jax import lax
from jax.experimental import pallas as pl
from jax.experimental.pallas import tpu as pltpu
from jax.sharding import PartitionSpec as P

EPSILON = 1e-06
TILE = 128
CHUNK = 2 * TILE


def passed_along(value, axis, steps):
    count = lax.axis_size(axis)
    pairs = [(source, (source + steps) % count) for source in range(count)]
    return lax.ppermute(value, axis, pairs)


def ring_body(embeddings, head_weight, gp_weights, counts):
    enc_size = lax.axis_size("enc")
    rep_size = lax.axis_size("rep")
    loop_size = lax.axis_size("loop")
    share_rows = embeddings.shape[0]
    piece_rows = share_rows // enc_size
    block_rows = share_rows * rep_size
    loop_index = lax.axis_index("loop")
    enc_index = lax.axis_index("enc")
    rep_index = lax.axis_index("rep")
    own_feats = lax.psum_scatter(
        jnp.dot(embeddings, head_weight, preferred_element_type=jnp.float32),
        "enc",
        scatter_dimension=0,
        tiled=True,
    ).astype(jnp.bfloat16)
    block_feats = lax.all_gather(own_feats, ("enc", "rep"), axis=0, tiled=True)
    block_norms = jnp.sum(jnp.square(block_feats.astype(jnp.float32)), axis=1)
    offsets = (
        jnp.arange(rep_size, dtype=jnp.int32)[None, :, None] * share_rows
        + jnp.arange(enc_size, dtype=jnp.int32)[:, None, None] * piece_rows
        + jnp.arange(piece_rows, dtype=jnp.int32)[None, None, :]
    ).reshape(block_rows)
    own_base = lax.dynamic_slice_in_dim(gp_weights, loop_index * block_rows, block_rows)
    block_coef = (
        own_base.reshape(rep_size, enc_size, piece_rows).transpose(1, 0, 2).reshape(block_rows)
    )
    own_count = lax.dynamic_index_in_dim(counts, loop_index, keepdims=False)
    block_coef = jnp.where(offsets < own_count, block_coef, 0.0)
    piece_start = rep_index * share_rows + enc_index * piece_rows
    piece_offsets = piece_start + jnp.arange(piece_rows, dtype=jnp.int32)

    def tile(state, piece, anchor):
        anchor_count = lax.dynamic_index_in_dim(counts, anchor, keepdims=False)
        accum, quotient_sum = state
        piece_coef = lax.dynamic_slice_in_dim(
            gp_weights, anchor * block_rows + piece_start, piece_rows
        )
        piece_coef = jnp.where(piece_offsets < anchor_count, piece_coef, 0.0)
        piece_norms = jnp.sum(jnp.square(piece.astype(jnp.float32)), axis=1)
        scores = lax.dot_general(
            piece, block_feats, (((1,), (1,)), ((), ())), preferred_element_type=jnp.float32
        )
        denom = piece_norms[:, None] + block_norms[None, :] - scores + EPSILON
        inverse = 1.0 / (denom * denom)
        pair_coef = piece_coef[:, None] * block_coef[None, :]
        pair_weight = (pair_coef * (piece_norms[:, None] + block_norms[None, :]) * inverse).astype(
            jnp.bfloat16
        )
        quotient_sum = quotient_sum + jnp.sum(pair_coef * 2.0 * scores * inverse, axis=0)
        accum = accum + lax.dot_general(
            pair_weight, piece, (((0,), (0,)), ((), ())), preferred_element_type=jnp.float32
        )
        return (accum, quotient_sum)

    start_state = (
        jnp.zeros((block_rows, block_feats.shape[1]), jnp.float32),
        jnp.zeros((block_rows,), jnp.float32),
    )
    state = tile(start_state, own_feats, loop_index)

    def forward_step(step_index, carry):
        moving, inner = carry
        moving = passed_along(moving, "loop", 1)
        inner = tile(inner, moving, (loop_index - step_index - 1 + loop_size) % loop_size)
        return (moving, inner)

    moving, state = lax.fori_loop(0, loop_size - 1, forward_step, (own_feats, state))
    accum, quotient_sum = state
    grad_block = accum - block_feats.astype(jnp.float32) * quotient_sum[:, None]
    own_grad = lax.psum_scatter(
        grad_block.astype(jnp.bfloat16), ("enc", "rep"), scatter_dimension=0, tiled=True
    )
    piece = lax.all_gather(own_grad, "enc", axis=0, tiled=True)
    embed_part = lax.dot_general(
        piece, head_weight, (((1,), (1,)), ((), ())), preferred_element_type=jnp.float32
    )
    head_part = lax.dot_general(
        embeddings, piece, (((0,), (0,)), ((), ())), preferred_element_type=jnp.float32
    )
    head_grad = lax.psum(head_part, ("loop", "rep"))
    return (embed_part.astype(jnp.bfloat16), head_grad)


OWN_ORDER = ((0, 0), (0, 1), (2, 0), (2, 1), (3, 1), (3, 0), (1, 1), (1, 0))
SLOTS = [(0, k, h) for k, h in OWN_ORDER] + [(1, k, h) for k, h in OWN_ORDER[::-1]]
LENT = ((1, 0), (1, 1), (3, 0), (3, 1))
PLACES = 24


def turned(row):
    return jnp.transpose(jnp.broadcast_to(row, (TILE, TILE)))[:, :1]


def prep_kernel(counts_ref, gp_ref, weights, places):
    z = lax.axis_index("loop")
    rep = lax.axis_index("rep")
    lane = lax.broadcasted_iota(jnp.int32, (1, TILE), 1)
    weights[...] = jnp.zeros_like(weights)
    total = jnp.int32(0)
    totals = []
    for slot, (other, k, h) in enumerate(SLOTS):
        block = jnp.bitwise_xor(z, k)
        piece = rep if other == 0 else 1 - rep
        base = piece * (2 * TILE) + h * TILE
        count = counts_ref[block]
        valid = count > base

        @pl.when(valid)
        def _(block=block, piece=piece, h=h, base=base, count=count, total=total):
            row = gp_ref[pl.ds(block * 4 + piece * 2 + h, 1), :]
            weights[pl.ds(total, 1), :] = jnp.where(lane + base < count, row, 0.0)

        places[slot] = jnp.where(valid, total, -1)
        total = total + valid.astype(jnp.int32)
        totals.append(total)
    own = totals[len(OWN_ORDER) - 1]
    places[16] = total
    places[17] = jnp.where(rep == 0, (total + 1) // 2, total // 2)
    places[18] = jnp.clip(counts_ref[z] - rep * (2 * TILE), 0, 2 * TILE)
    places[19] = own


def tile_at(place):
    return pl.ds(pl.multiple_of(place * TILE, TILE), TILE)


def pack_tiles(distances, places, own_feats, other_feats, own_near, lent, feats, norms, near):
    width = feats.shape[1]
    for slot, (other, k, h) in enumerate(SLOTS):
        if k not in distances:
            continue
        place = places[slot]

        @pl.when(place >= 0)
        def _(place=place, other=other, k=k, h=h):
            here = slice(h * TILE, (h + 1) * TILE)
            value = (other_feats if other else own_feats)[k][here, :]
            feats[tile_at(place), :] = value
            wide = value.astype(jnp.float32)
            square = wide * wide
            part = square[:, :TILE]
            for s in range(1, width // TILE):
                part += square[:, s * TILE : (s + 1) * TILE]
            norms[pl.ds(place, 1), :] = jnp.sum(jnp.transpose(part), axis=0, keepdims=True)
            if other == 0:
                near[tile_at(place), :] = own_near[k][here, :]
            elif (k, h) in LENT:
                near[tile_at(place), :] = lent[k][here, :]


def pack_kernel(places, near0, near1, lent1, own0, own1, other0, other1, feats, norms, near):
    pack_tiles(
        (0, 1),
        places,
        {0: own0, 1: own1},
        {0: other0, 1: other1},
        {0: near0, 1: near1},
        {1: lent1},
        feats,
        norms,
        near,
    )


def pair_kernel(
    places,
    weights,
    near2,
    near3,
    lent3,
    own2,
    own3,
    other2,
    other3,
    feats_in,
    norms_in,
    near_in,
    feats,
    norms,
    near,
    own_out,
    head_out,
    grads,
):
    del feats_in, norms_in, near_in
    width = feats.shape[1]
    total, rows_here, own_valid = places[16], places[17], places[18]
    pack_tiles(
        (2, 3),
        places,
        {2: own2, 3: own3},
        {2: other2, 3: other3},
        {2: near2, 3: near3},
        {3: lent3},
        feats,
        norms,
        near,
    )
    feats[tile_at(total), :] = jnp.zeros((TILE, width), jnp.bfloat16)
    norms[pl.ds(total, 1), :] = jnp.zeros((1, TILE), jnp.float32)

    def row_chunk(i, tiles):
        rows = pl.ds(pl.multiple_of(i * CHUNK, CHUNK), CHUNK)
        left = feats[rows, :]
        right = feats[: tiles * TILE, :]
        pair_of = [pl.ds(2 * i, 1), pl.ds(2 * i + 1, 1)]
        left_norms = jnp.concatenate([turned(norms[at, :]) for at in pair_of], axis=0)
        coef = jnp.concatenate([turned(weights[at, :]) for at in pair_of], axis=0)
        scores = lax.dot_general(
            left, right, (((1,), (1,)), ((), ())), preferred_element_type=jnp.float32
        )
        all_norms = jnp.concatenate([norms[t : t + 1, :] for t in range(tiles)], axis=1)
        all_coef = jnp.concatenate([weights[t : t + 1, :] for t in range(tiles)], axis=1)
        both = left_norms + all_norms
        denom = both - scores + EPSILON
        scaled = all_coef * (1.0 / (denom * denom))
        pair = (scaled * both).astype(jnp.bfloat16)
        quotient = 2.0 * jnp.sum(scaled * scores, axis=1, keepdims=True)
        carried = jnp.dot(pair, right, preferred_element_type=jnp.float32)
        row = lax.broadcasted_iota(jnp.int32, (CHUNK, 1), 0) + i * CHUNK
        coef = jnp.where(row < rows_here * TILE, coef, 0.0)
        grad = coef * (carried - left.astype(jnp.float32) * quotient)
        grads[rows, :] = grad.astype(jnp.bfloat16)

    chunks = (rows_here + 1) // 2
    behind = 2 * chunks - 1

    @pl.when(behind >= rows_here)
    def _():
        near[tile_at(behind), :] = jnp.zeros((TILE, near.shape[1]), near.dtype)

    col_tiles = jnp.maximum(2 * ((total + 1) // 2), 8)
    for tiles in (8, 10, 12, 14):

        @pl.when(col_tiles == tiles)
        def _(tiles=tiles):
            def step(i, _):
                row_chunk(i, tiles)
                return 0

            lax.fori_loop(0, chunks, step, 0)

    for count in (1, 2, 3, 4):

        @pl.when(chunks == count)
        def _(count=count):
            rows = slice(0, count * CHUNK)
            head_out[...] = lax.dot_general(
                near[rows, :],
                grads[rows, :],
                (((0,), (0,)), ((), ())),
                preferred_element_type=jnp.float32,
            )

    own = grads[:CHUNK, :]
    row = lax.broadcasted_iota(jnp.int32, (CHUNK, 1), 0)
    own_out[...] = jnp.where(row < own_valid, own, jnp.zeros_like(own))


def gathered_body(embeddings, head_weight, gp_weights, counts):
    loop_size = lax.axis_size("loop")
    rep = lax.axis_index("rep")
    share_rows, share_cols = embeddings.shape
    enc_rows, width = head_weight.shape

    def across_z(value, step):
        return lax.ppermute(value, "loop", [(i, i ^ step) for i in range(loop_size)])

    def across_x(value):
        return lax.ppermute(value, "enc", [(0, 1), (1, 0)])

    def across_cores(value):
        return lax.ppermute(value, "rep", [(0, 1), (1, 0)])

    def after(value, *others):
        return lax.optimization_barrier((value, *others))[0]

    smem = pl.BlockSpec(memory_space=pltpu.SMEM)
    vmem = pl.BlockSpec(memory_space=pltpu.VMEM)
    weights, places = pl.pallas_call(
        prep_kernel,
        out_shape=(
            jax.ShapeDtypeStruct((PLACES, TILE), jnp.float32),
            jax.ShapeDtypeStruct((PLACES,), jnp.int32),
        ),
        in_specs=[smem, vmem],
        out_specs=(vmem, smem),
    )(counts, gp_weights.reshape(-1, TILE))

    far0 = across_x(embeddings)
    near3 = across_z(embeddings, 3)
    near1 = across_z(embeddings, 1)
    half = enc_rows // 2
    head_mine = across_x(lax.dynamic_slice_in_dim(head_weight, rep * half, half, 0))
    head_other = across_cores(head_mine)
    far_head = jnp.where(
        rep == 0,
        jnp.concatenate([head_mine, head_other]),
        jnp.concatenate([head_other, head_mine]),
    )
    far0_next, weights, places = lax.optimization_barrier((far0, weights, places))
    near3, far_head = lax.optimization_barrier((near3, far_head))
    far2 = across_z(far0_next, 2)
    near2 = across_z(near3, 1)
    far1 = across_x(near1)
    far3 = across_x(near3)

    def features(near, far):
        value = jnp.dot(near, head_weight, preferred_element_type=jnp.float32)
        value += jnp.dot(far, far_head, preferred_element_type=jnp.float32)
        return value.astype(jnp.bfloat16)

    own0, own1 = features(embeddings, far0), features(near1, far1)
    other0, other1 = across_cores(own0), across_cores(own1)
    lent1 = across_cores(after(near1, own1))
    buffers = (
        jax.ShapeDtypeStruct((18 * TILE, width), jnp.bfloat16),
        jax.ShapeDtypeStruct((PLACES, TILE), jnp.float32),
        jax.ShapeDtypeStruct((12 * TILE, share_cols), jnp.bfloat16),
    )
    packed = pl.pallas_call(
        pack_kernel,
        out_shape=buffers,
        in_specs=[smem] + [vmem] * 7,
        out_specs=(vmem,) * 3,
        compiler_params=pltpu.CompilerParams(vmem_limit_bytes=30 * 2**20),
    )(places, embeddings, near1, lent1, own0, own1, other0, other1)

    own2, own3 = features(near2, far2), features(near3, far3)
    other2, other3 = across_cores(own2), across_cores(own3)
    lent3 = across_cores(after(near3, own3))

    *_, own_grad, head_part = pl.pallas_call(
        pair_kernel,
        out_shape=buffers
        + (
            jax.ShapeDtypeStruct((share_rows, width), jnp.bfloat16),
            jax.ShapeDtypeStruct((enc_rows, width), jnp.float32),
        ),
        in_specs=[smem] + [vmem] * 11,
        out_specs=(vmem,) * 5,
        input_output_aliases={9: 0, 10: 1, 11: 2},
        scratch_shapes=[pltpu.VMEM((4 * CHUNK, width), jnp.bfloat16)],
        compiler_params=pltpu.CompilerParams(vmem_limit_bytes=40 * 2**20),
    )(places, weights, near2, near3, lent3, own2, own3, other2, other3, *packed)
    head_other_part = across_cores(head_part)
    embed_grad = lax.dot_general(
        own_grad, head_weight, (((1,), (1,)), ((), ())), preferred_element_type=jnp.float32
    ).astype(jnp.bfloat16)
    return embed_grad, head_part + head_other_part


def solution(mesh):
    placed = (P(("groups", "loop", "rep"), "enc"), P("enc", None), P("groups"), P("groups"))
    sizes = dict(mesh.shape)

    def body(*arrays):
        share_rows = arrays[0].shape[0]
        small = sizes["loop"] == 4 and sizes["enc"] == 2 and sizes["rep"] == 2
        if small and share_rows == 2 * TILE:
            return gathered_body(*arrays)
        return ring_body(*arrays)

    return jax.shard_map(
        body,
        mesh=mesh,
        in_specs=placed,
        out_specs=(P(("groups", "loop", "rep"), "enc"), P(("groups", "enc"), None)),
        check_vma=False,
    )
```

```python
import jax
import jax.numpy as jnp
from jax import lax
from jax.experimental import pallas as pl
from jax.experimental.pallas import tpu as pltpu
from jax.sharding import PartitionSpec as P

EPSILON = 1e-06
TILE = 128
CHUNK = 2 * TILE


def passed_along(value, axis, steps):
    count = lax.axis_size(axis)
    pairs = [(source, (source + steps) % count) for source in range(count)]
    return lax.ppermute(value, axis, pairs)


def ring_body(embeddings, head_weight, gp_weights, counts):
    enc_size = lax.axis_size("enc")
    rep_size = lax.axis_size("rep")
    loop_size = lax.axis_size("loop")
    share_rows = embeddings.shape[0]
    piece_rows = share_rows // enc_size
    block_rows = share_rows * rep_size
    loop_index = lax.axis_index("loop")
    enc_index = lax.axis_index("enc")
    rep_index = lax.axis_index("rep")
    own_feats = lax.psum_scatter(
        jnp.dot(embeddings, head_weight, preferred_element_type=jnp.float32),
        "enc",
        scatter_dimension=0,
        tiled=True,
    ).astype(jnp.bfloat16)
    block_feats = lax.all_gather(own_feats, ("enc", "rep"), axis=0, tiled=True)
    block_norms = jnp.sum(jnp.square(block_feats.astype(jnp.float32)), axis=1)
    offsets = (
        jnp.arange(rep_size, dtype=jnp.int32)[None, :, None] * share_rows
        + jnp.arange(enc_size, dtype=jnp.int32)[:, None, None] * piece_rows
        + jnp.arange(piece_rows, dtype=jnp.int32)[None, None, :]
    ).reshape(block_rows)
    own_base = lax.dynamic_slice_in_dim(gp_weights, loop_index * block_rows, block_rows)
    block_coef = (
        own_base.reshape(rep_size, enc_size, piece_rows).transpose(1, 0, 2).reshape(block_rows)
    )
    own_count = lax.dynamic_index_in_dim(counts, loop_index, keepdims=False)
    block_coef = jnp.where(offsets < own_count, block_coef, 0.0)
    piece_start = rep_index * share_rows + enc_index * piece_rows
    piece_offsets = piece_start + jnp.arange(piece_rows, dtype=jnp.int32)

    def tile(state, piece, anchor):
        anchor_count = lax.dynamic_index_in_dim(counts, anchor, keepdims=False)
        accum, quotient_sum = state
        piece_coef = lax.dynamic_slice_in_dim(
            gp_weights, anchor * block_rows + piece_start, piece_rows
        )
        piece_coef = jnp.where(piece_offsets < anchor_count, piece_coef, 0.0)
        piece_norms = jnp.sum(jnp.square(piece.astype(jnp.float32)), axis=1)
        scores = lax.dot_general(
            piece, block_feats, (((1,), (1,)), ((), ())), preferred_element_type=jnp.float32
        )
        denom = piece_norms[:, None] + block_norms[None, :] - scores + EPSILON
        inverse = 1.0 / (denom * denom)
        pair_coef = piece_coef[:, None] * block_coef[None, :]
        pair_weight = (pair_coef * (piece_norms[:, None] + block_norms[None, :]) * inverse).astype(
            jnp.bfloat16
        )
        quotient_sum = quotient_sum + jnp.sum(pair_coef * 2.0 * scores * inverse, axis=0)
        accum = accum + lax.dot_general(
            pair_weight, piece, (((0,), (0,)), ((), ())), preferred_element_type=jnp.float32
        )
        return (accum, quotient_sum)

    start_state = (
        jnp.zeros((block_rows, block_feats.shape[1]), jnp.float32),
        jnp.zeros((block_rows,), jnp.float32),
    )
    state = tile(start_state, own_feats, loop_index)

    def forward_step(step_index, carry):
        moving, inner = carry
        moving = passed_along(moving, "loop", 1)
        inner = tile(inner, moving, (loop_index - step_index - 1 + loop_size) % loop_size)
        return (moving, inner)

    moving, state = lax.fori_loop(0, loop_size - 1, forward_step, (own_feats, state))
    accum, quotient_sum = state
    grad_block = accum - block_feats.astype(jnp.float32) * quotient_sum[:, None]
    own_grad = lax.psum_scatter(
        grad_block.astype(jnp.bfloat16), ("enc", "rep"), scatter_dimension=0, tiled=True
    )
    piece = lax.all_gather(own_grad, "enc", axis=0, tiled=True)
    embed_part = lax.dot_general(
        piece, head_weight, (((1,), (1,)), ((), ())), preferred_element_type=jnp.float32
    )
    head_part = lax.dot_general(
        embeddings, piece, (((0,), (0,)), ((), ())), preferred_element_type=jnp.float32
    )
    head_grad = lax.psum(head_part, ("loop", "rep"))
    return (embed_part.astype(jnp.bfloat16), head_grad)


OWN_ORDER = ((0, 0), (0, 1), (2, 0), (2, 1), (3, 1), (3, 0), (1, 1), (1, 0))
SLOTS = [(0, k, h) for k, h in OWN_ORDER] + [(1, k, h) for k, h in OWN_ORDER[::-1]]
LENT = ((1, 0), (1, 1), (3, 0), (3, 1))
PLACES = 24


def turned(row):
    return jnp.transpose(jnp.broadcast_to(row, (TILE, TILE)))[:, :1]


def prep_kernel(counts_ref, gp_ref, weights, places):
    z = lax.axis_index("loop")
    rep = lax.axis_index("rep")
    lane = lax.broadcasted_iota(jnp.int32, (1, TILE), 1)
    weights[...] = jnp.zeros_like(weights)
    total = jnp.int32(0)
    totals = []
    for slot, (other, k, h) in enumerate(SLOTS):
        block = jnp.bitwise_xor(z, k)
        piece = rep if other == 0 else 1 - rep
        base = piece * (2 * TILE) + h * TILE
        count = counts_ref[block]
        valid = count > base

        @pl.when(valid)
        def _(block=block, piece=piece, h=h, base=base, count=count, total=total):
            row = gp_ref[pl.ds(block * 4 + piece * 2 + h, 1), :]
            weights[pl.ds(total, 1), :] = jnp.where(lane + base < count, row, 0.0)

        places[slot] = jnp.where(valid, total, -1)
        total = total + valid.astype(jnp.int32)
        totals.append(total)
    own = totals[len(OWN_ORDER) - 1]
    places[16] = total
    places[17] = jnp.where(rep == 0, (total + 1) // 2, total // 2)
    places[18] = jnp.clip(counts_ref[z] - rep * (2 * TILE), 0, 2 * TILE)
    places[19] = own


def tile_at(place):
    return pl.ds(pl.multiple_of(place * TILE, TILE), TILE)


def pack_tiles(places, pieces, rows_of, feats, norms, near):
    width = feats.shape[1]
    for slot, (other, k, h) in enumerate(SLOTS):
        if (other, k) not in pieces:
            continue
        place = places[slot]

        @pl.when(place >= 0)
        def _(place=place, other=other, k=k, h=h):
            here = slice(h * TILE, (h + 1) * TILE)
            value = pieces[other, k][here, :]
            feats[tile_at(place), :] = value
            wide = value.astype(jnp.float32)
            square = wide * wide
            part = square[:, :TILE]
            for s in range(1, width // TILE):
                part += square[:, s * TILE : (s + 1) * TILE]
            norms[pl.ds(place, 1), :] = jnp.sum(jnp.transpose(part), axis=0, keepdims=True)
            if (other, k) in rows_of:
                near[tile_at(place), :] = rows_of[other, k][here, :]


def pack_kernel(
    places,
    near0,
    near1,
    near2,
    near3,
    lent1,
    own0,
    own1,
    own2,
    own3,
    other0,
    other1,
    feats,
    norms,
    near,
):
    pieces = {
        (0, 0): own0,
        (0, 1): own1,
        (0, 2): own2,
        (0, 3): own3,
        (1, 0): other0,
        (1, 1): other1,
    }
    rows_of = {(0, 0): near0, (0, 1): near1, (0, 2): near2, (0, 3): near3, (1, 1): lent1}
    pack_tiles(places, pieces, rows_of, feats, norms, near)


def pair_kernel(
    places,
    weights,
    lent3,
    other2,
    other3,
    feats_in,
    norms_in,
    near_in,
    feats,
    norms,
    near,
    own_out,
    head_out,
    head_sent,
    grads,
):
    del feats_in, norms_in, near_in
    width = feats.shape[1]
    total, rows_here, own_valid = places[16], places[17], places[18]
    pack_tiles(
        places, {(1, 2): other2, (1, 3): other3}, {(1, 3): lent3}, feats, norms, near
    )
    feats[tile_at(total), :] = jnp.zeros((TILE, width), jnp.bfloat16)
    norms[pl.ds(total, 1), :] = jnp.zeros((1, TILE), jnp.float32)

    def row_chunk(i, tiles):
        rows = pl.ds(pl.multiple_of(i * CHUNK, CHUNK), CHUNK)
        left = feats[rows, :]
        right = feats[: tiles * TILE, :]
        pair_of = [pl.ds(2 * i, 1), pl.ds(2 * i + 1, 1)]
        left_norms = jnp.concatenate([turned(norms[at, :]) for at in pair_of], axis=0)
        coef = jnp.concatenate([turned(weights[at, :]) for at in pair_of], axis=0)
        scores = lax.dot_general(
            left, right, (((1,), (1,)), ((), ())), preferred_element_type=jnp.float32
        )
        all_norms = jnp.concatenate([norms[t : t + 1, :] for t in range(tiles)], axis=1)
        all_coef = jnp.concatenate([weights[t : t + 1, :] for t in range(tiles)], axis=1)
        both = left_norms + all_norms
        denom = both - scores + EPSILON
        scaled = all_coef * (1.0 / (denom * denom))
        pair = (scaled * both).astype(jnp.bfloat16)
        quotient = 2.0 * jnp.sum(scaled * scores, axis=1, keepdims=True)
        carried = jnp.dot(pair, right, preferred_element_type=jnp.float32)
        row = lax.broadcasted_iota(jnp.int32, (CHUNK, 1), 0) + i * CHUNK
        coef = jnp.where(row < rows_here * TILE, coef, 0.0)
        grad = coef * (carried - left.astype(jnp.float32) * quotient)
        grads[rows, :] = grad.astype(jnp.bfloat16)

    chunks = (rows_here + 1) // 2
    behind = 2 * chunks - 1

    @pl.when(behind >= rows_here)
    def _():
        near[tile_at(behind), :] = jnp.zeros((TILE, near.shape[1]), near.dtype)

    col_tiles = jnp.maximum(2 * ((total + 1) // 2), 8)
    for tiles in (8, 10, 12, 14):

        @pl.when(col_tiles == tiles)
        def _(tiles=tiles):
            def step(i, _):
                row_chunk(i, tiles)
                return 0

            lax.fori_loop(0, chunks, step, 0)

    for count in (1, 2, 3, 4):

        @pl.when(chunks == count)
        def _(count=count):
            rows = slice(0, count * CHUNK)
            head = lax.dot_general(
                near[rows, :],
                grads[rows, :],
                (((0,), (0,)), ((), ())),
                preferred_element_type=jnp.float32,
            )
            head_out[...] = head
            head_sent[...] = head.astype(jnp.bfloat16)

    own = grads[:CHUNK, :]
    row = lax.broadcasted_iota(jnp.int32, (CHUNK, 1), 0)
    own_out[...] = jnp.where(row < own_valid, own, jnp.zeros_like(own))


def gathered_body(embeddings, head_weight, gp_weights, counts):
    loop_size = lax.axis_size("loop")
    rep = lax.axis_index("rep")
    share_rows, share_cols = embeddings.shape
    enc_rows, width = head_weight.shape

    def across_z(value, step):
        return lax.ppermute(value, "loop", [(i, i ^ step) for i in range(loop_size)])

    def across_x(value):
        return lax.ppermute(value, "enc", [(0, 1), (1, 0)])

    def across_cores(value):
        return lax.ppermute(value, "rep", [(0, 1), (1, 0)])

    def after(value, *others):
        return lax.optimization_barrier((value, *others))[0]

    smem = pl.BlockSpec(memory_space=pltpu.SMEM)
    vmem = pl.BlockSpec(memory_space=pltpu.VMEM)
    weights, places = pl.pallas_call(
        prep_kernel,
        out_shape=(
            jax.ShapeDtypeStruct((PLACES, TILE), jnp.float32),
            jax.ShapeDtypeStruct((PLACES,), jnp.int32),
        ),
        in_specs=[smem, vmem],
        out_specs=(vmem, smem),
    )(counts, gp_weights.reshape(-1, TILE))

    far0 = across_x(embeddings)
    near3 = across_z(embeddings, 3)
    near1 = across_z(embeddings, 1)
    half = enc_rows // 2
    head_mine = across_x(lax.dynamic_slice_in_dim(head_weight, rep * half, half, 0))
    head_other = across_cores(head_mine)
    far_head = jnp.where(
        rep == 0,
        jnp.concatenate([head_mine, head_other]),
        jnp.concatenate([head_other, head_mine]),
    )
    far0_next, weights, places = lax.optimization_barrier((far0, weights, places))
    near3, far_head = lax.optimization_barrier((near3, far_head))
    far2 = across_z(far0_next, 2)
    near2 = across_z(near3, 1)
    far1 = across_x(near1)
    far3 = across_x(near3)

    def features(near, far):
        value = jnp.dot(near, head_weight, preferred_element_type=jnp.float32)
        value += jnp.dot(far, far_head, preferred_element_type=jnp.float32)
        return value.astype(jnp.bfloat16)

    own0, own1 = features(embeddings, far0), features(near1, far1)
    other0, other1 = across_cores(own0), across_cores(own1)
    lent1 = across_cores(after(near1, own1))
    buffers = (
        jax.ShapeDtypeStruct((18 * TILE, width), jnp.bfloat16),
        jax.ShapeDtypeStruct((PLACES, TILE), jnp.float32),
        jax.ShapeDtypeStruct((12 * TILE, share_cols), jnp.bfloat16),
    )
    own2, own3 = features(near2, far2), features(near3, far3)
    other2, other3 = across_cores(own2), across_cores(own3)
    lent3 = across_cores(after(near3, own3))
    packed = pl.pallas_call(
        pack_kernel,
        out_shape=buffers,
        in_specs=[smem] + [vmem] * 11,
        out_specs=(vmem,) * 3,
        compiler_params=pltpu.CompilerParams(vmem_limit_bytes=30 * 2**20),
    )(
        places,
        embeddings,
        near1,
        near2,
        near3,
        lent1,
        own0,
        own1,
        own2,
        own3,
        other0,
        other1,
    )

    *_, own_grad, head_part, head_sent = pl.pallas_call(
        pair_kernel,
        out_shape=buffers
        + (
            jax.ShapeDtypeStruct((share_rows, width), jnp.bfloat16),
            jax.ShapeDtypeStruct((enc_rows, width), jnp.float32),
            jax.ShapeDtypeStruct((enc_rows, width), jnp.bfloat16),
        ),
        in_specs=[smem] + [vmem] * 7,
        out_specs=(vmem,) * 6,
        input_output_aliases={5: 0, 6: 1, 7: 2},
        scratch_shapes=[pltpu.VMEM((4 * CHUNK, width), jnp.bfloat16)],
        compiler_params=pltpu.CompilerParams(vmem_limit_bytes=40 * 2**20),
    )(places, weights, lent3, other2, other3, *packed)
    head_other_part = across_cores(head_sent)
    embed_grad = lax.dot_general(
        own_grad, head_weight, (((1,), (1,)), ((), ())), preferred_element_type=jnp.float32
    ).astype(jnp.bfloat16)
    head_grad = head_part + head_other_part.astype(jnp.float32)
    return embed_grad, head_grad


def solution(mesh):
    placed = (P(("groups", "loop", "rep"), "enc"), P("enc", None), P("groups"), P("groups"))
    sizes = dict(mesh.shape)

    def body(*arrays):
        share_rows = arrays[0].shape[0]
        small = sizes["loop"] == 4 and sizes["enc"] == 2 and sizes["rep"] == 2
        if small and share_rows == 2 * TILE:
            return gathered_body(*arrays)
        return ring_body(*arrays)

    return jax.shard_map(
        body,
        mesh=mesh,
        in_specs=placed,
        out_specs=(P(("groups", "loop", "rep"), "enc"), P(("groups", "enc"), None)),
        check_vma=False,
    )
```

```python
import jax
import jax.numpy as jnp
from jax import lax
from jax.experimental import pallas as pl
from jax.experimental.pallas import tpu as pltpu
from jax.sharding import PartitionSpec as P

EPSILON = 1e-06
TILE = 128
CHUNK = 2 * TILE


def passed_along(value, axis, steps):
    count = lax.axis_size(axis)
    pairs = [(source, (source + steps) % count) for source in range(count)]
    return lax.ppermute(value, axis, pairs)


def ring_body(embeddings, head_weight, gp_weights, counts):
    enc_size = lax.axis_size("enc")
    rep_size = lax.axis_size("rep")
    loop_size = lax.axis_size("loop")
    share_rows = embeddings.shape[0]
    piece_rows = share_rows // enc_size
    block_rows = share_rows * rep_size
    loop_index = lax.axis_index("loop")
    enc_index = lax.axis_index("enc")
    rep_index = lax.axis_index("rep")
    own_feats = lax.psum_scatter(
        jnp.dot(embeddings, head_weight, preferred_element_type=jnp.float32),
        "enc",
        scatter_dimension=0,
        tiled=True,
    ).astype(jnp.bfloat16)
    block_feats = lax.all_gather(own_feats, ("enc", "rep"), axis=0, tiled=True)
    block_norms = jnp.sum(jnp.square(block_feats.astype(jnp.float32)), axis=1)
    offsets = (
        jnp.arange(rep_size, dtype=jnp.int32)[None, :, None] * share_rows
        + jnp.arange(enc_size, dtype=jnp.int32)[:, None, None] * piece_rows
        + jnp.arange(piece_rows, dtype=jnp.int32)[None, None, :]
    ).reshape(block_rows)
    own_base = lax.dynamic_slice_in_dim(gp_weights, loop_index * block_rows, block_rows)
    block_coef = (
        own_base.reshape(rep_size, enc_size, piece_rows).transpose(1, 0, 2).reshape(block_rows)
    )
    own_count = lax.dynamic_index_in_dim(counts, loop_index, keepdims=False)
    block_coef = jnp.where(offsets < own_count, block_coef, 0.0)
    piece_start = rep_index * share_rows + enc_index * piece_rows
    piece_offsets = piece_start + jnp.arange(piece_rows, dtype=jnp.int32)

    def tile(state, piece, anchor):
        anchor_count = lax.dynamic_index_in_dim(counts, anchor, keepdims=False)
        accum, quotient_sum = state
        piece_coef = lax.dynamic_slice_in_dim(
            gp_weights, anchor * block_rows + piece_start, piece_rows
        )
        piece_coef = jnp.where(piece_offsets < anchor_count, piece_coef, 0.0)
        piece_norms = jnp.sum(jnp.square(piece.astype(jnp.float32)), axis=1)
        scores = lax.dot_general(
            piece, block_feats, (((1,), (1,)), ((), ())), preferred_element_type=jnp.float32
        )
        denom = piece_norms[:, None] + block_norms[None, :] - scores + EPSILON
        inverse = 1.0 / (denom * denom)
        pair_coef = piece_coef[:, None] * block_coef[None, :]
        pair_weight = (pair_coef * (piece_norms[:, None] + block_norms[None, :]) * inverse).astype(
            jnp.bfloat16
        )
        quotient_sum = quotient_sum + jnp.sum(pair_coef * 2.0 * scores * inverse, axis=0)
        accum = accum + lax.dot_general(
            pair_weight, piece, (((0,), (0,)), ((), ())), preferred_element_type=jnp.float32
        )
        return (accum, quotient_sum)

    start_state = (
        jnp.zeros((block_rows, block_feats.shape[1]), jnp.float32),
        jnp.zeros((block_rows,), jnp.float32),
    )
    state = tile(start_state, own_feats, loop_index)

    def forward_step(step_index, carry):
        moving, inner = carry
        moving = passed_along(moving, "loop", 1)
        inner = tile(inner, moving, (loop_index - step_index - 1 + loop_size) % loop_size)
        return (moving, inner)

    moving, state = lax.fori_loop(0, loop_size - 1, forward_step, (own_feats, state))
    accum, quotient_sum = state
    grad_block = accum - block_feats.astype(jnp.float32) * quotient_sum[:, None]
    own_grad = lax.psum_scatter(
        grad_block.astype(jnp.bfloat16), ("enc", "rep"), scatter_dimension=0, tiled=True
    )
    piece = lax.all_gather(own_grad, "enc", axis=0, tiled=True)
    embed_part = lax.dot_general(
        piece, head_weight, (((1,), (1,)), ((), ())), preferred_element_type=jnp.float32
    )
    head_part = lax.dot_general(
        embeddings, piece, (((0,), (0,)), ((), ())), preferred_element_type=jnp.float32
    )
    head_grad = lax.psum(head_part, ("loop", "rep"))
    return (embed_part.astype(jnp.bfloat16), head_grad)


OWN_ORDER = ((0, 0), (0, 1), (2, 0), (2, 1), (3, 1), (3, 0), (1, 1), (1, 0))
SLOTS = [(0, k, h) for k, h in OWN_ORDER] + [(1, k, h) for k, h in OWN_ORDER[::-1]]
LENT = ((1, 0), (1, 1), (3, 0), (3, 1))
PLACES = 24


def turned(row):
    return jnp.transpose(jnp.broadcast_to(row, (TILE, TILE)))[:, :1]


def prep_kernel(counts_ref, gp_ref, weights, places):
    z = lax.axis_index("loop")
    rep = lax.axis_index("rep")
    lane = lax.broadcasted_iota(jnp.int32, (1, TILE), 1)
    weights[...] = jnp.zeros_like(weights)
    total = jnp.int32(0)
    totals = []
    for slot, (other, k, h) in enumerate(SLOTS):
        block = jnp.bitwise_xor(z, k)
        piece = rep if other == 0 else 1 - rep
        base = piece * (2 * TILE) + h * TILE
        count = counts_ref[block]
        valid = count > base

        @pl.when(valid)
        def _(block=block, piece=piece, h=h, base=base, count=count, total=total):
            row = gp_ref[pl.ds(block * 4 + piece * 2 + h, 1), :]
            weights[pl.ds(total, 1), :] = jnp.where(lane + base < count, row, 0.0)

        places[slot] = jnp.where(valid, total, -1)
        total = total + valid.astype(jnp.int32)
        totals.append(total)
    own = totals[len(OWN_ORDER) - 1]
    places[16] = total
    places[17] = jnp.where(rep == 0, (total + 1) // 2, total // 2)
    places[18] = jnp.clip(counts_ref[z] - rep * (2 * TILE), 0, 2 * TILE)
    places[19] = own


def tile_at(place):
    return pl.ds(pl.multiple_of(place * TILE, TILE), TILE)


def pack_tiles(places, pieces, rows_of, feats, norms, near):
    width = feats.shape[1]
    for slot, (other, k, h) in enumerate(SLOTS):
        if (other, k) not in pieces:
            continue
        place = places[slot]

        @pl.when(place >= 0)
        def _(place=place, other=other, k=k, h=h):
            here = slice(h * TILE, (h + 1) * TILE)
            value = pieces[other, k][here, :]
            feats[tile_at(place), :] = value
            wide = value.astype(jnp.float32)
            square = wide * wide
            part = square[:, :TILE]
            for s in range(1, width // TILE):
                part += square[:, s * TILE : (s + 1) * TILE]
            norms[pl.ds(place, 1), :] = jnp.sum(jnp.transpose(part), axis=0, keepdims=True)
            if (other, k) in rows_of:
                near[tile_at(place), :] = rows_of[other, k][here, :]


def pack_kernel(
    places,
    near0,
    near1,
    near2,
    near3,
    lent1,
    own0,
    own1,
    own2,
    own3,
    other0,
    other1,
    feats,
    norms,
    near,
):
    pieces = {
        (0, 0): own0,
        (0, 1): own1,
        (0, 2): own2,
        (0, 3): own3,
        (1, 0): other0,
        (1, 1): other1,
    }
    rows_of = {(0, 0): near0, (0, 1): near1, (0, 2): near2, (0, 3): near3, (1, 1): lent1}
    pack_tiles(places, pieces, rows_of, feats, norms, near)


def pair_kernel(
    places,
    weights,
    lent3,
    other2,
    other3,
    feats_in,
    norms_in,
    near_in,
    feats,
    norms,
    near,
    own_out,
    head_out,
    head_sent,
    grads,
):
    del feats_in, norms_in, near_in
    width = feats.shape[1]
    total, rows_here, own_valid = places[16], places[17], places[18]
    pack_tiles(
        places, {(1, 2): other2, (1, 3): other3}, {(1, 3): lent3}, feats, norms, near
    )
    feats[tile_at(total), :] = jnp.zeros((TILE, width), jnp.bfloat16)
    norms[pl.ds(total, 1), :] = jnp.zeros((1, TILE), jnp.float32)

    def row_chunk(i, deep, tiles):
        size = deep * TILE
        rows = pl.ds(pl.multiple_of(i * size, TILE), size)
        left = feats[rows, :]
        right = feats[: tiles * TILE, :]
        places_of = [pl.ds(deep * i + t, 1) for t in range(deep)]
        left_norms = jnp.concatenate([turned(norms[at, :]) for at in places_of], axis=0)
        coef = jnp.concatenate([turned(weights[at, :]) for at in places_of], axis=0)
        scores = lax.dot_general(
            left, right, (((1,), (1,)), ((), ())), preferred_element_type=jnp.float32
        )
        all_norms = jnp.concatenate([norms[t : t + 1, :] for t in range(tiles)], axis=1)
        all_coef = jnp.concatenate([weights[t : t + 1, :] for t in range(tiles)], axis=1)
        both = left_norms + all_norms
        denom = both - scores + EPSILON
        scaled = all_coef * (1.0 / (denom * denom))
        pair = (scaled * both).astype(jnp.bfloat16)
        quotient = 2.0 * jnp.sum(scaled * scores, axis=1, keepdims=True)
        carried = jnp.dot(pair, right, preferred_element_type=jnp.float32)
        row = lax.broadcasted_iota(jnp.int32, (size, 1), 0) + i * size
        coef = jnp.where(row < rows_here * TILE, coef, 0.0)
        grad = coef * (carried - left.astype(jnp.float32) * quotient)
        grads[rows, :] = grad.astype(jnp.bfloat16)

    row_tiles = jnp.maximum(2 * ((rows_here + 1) // 2), 4)

    @pl.when(row_tiles > rows_here)
    def _():
        near[tile_at(row_tiles - 1), :] = jnp.zeros((TILE, near.shape[1]), near.dtype)

    col_tiles = jnp.maximum(2 * ((total + 1) // 2), 8)
    for count, deep, columns in ((4, 2, (8, 10)), (6, 3, (10, 12, 14)), (8, 2, (14,))):
        for tiles in columns:

            @pl.when(jnp.logical_and(col_tiles == tiles, row_tiles == count))
            def _(count=count, deep=deep, tiles=tiles):
                def step(i, _):
                    row_chunk(i, deep, tiles)
                    return 0

                lax.fori_loop(0, count // deep, step, 0)

        @pl.when(row_tiles == count)
        def _(count=count):
            rows = slice(0, count * TILE)
            head = lax.dot_general(
                near[rows, :],
                grads[rows, :],
                (((0,), (0,)), ((), ())),
                preferred_element_type=jnp.float32,
            )
            head_out[...] = head
            head_sent[...] = head.astype(jnp.bfloat16)

    own = grads[:CHUNK, :]
    row = lax.broadcasted_iota(jnp.int32, (CHUNK, 1), 0)
    own_out[...] = jnp.where(row < own_valid, own, jnp.zeros_like(own))


def gathered_body(embeddings, head_weight, gp_weights, counts):
    loop_size = lax.axis_size("loop")
    rep = lax.axis_index("rep")
    share_rows, share_cols = embeddings.shape
    enc_rows, width = head_weight.shape

    def across_z(value, step):
        return lax.ppermute(value, "loop", [(i, i ^ step) for i in range(loop_size)])

    def across_x(value):
        return lax.ppermute(value, "enc", [(0, 1), (1, 0)])

    def across_cores(value):
        return lax.ppermute(value, "rep", [(0, 1), (1, 0)])

    def after(value, *others):
        return lax.optimization_barrier((value, *others))[0]

    smem = pl.BlockSpec(memory_space=pltpu.SMEM)
    vmem = pl.BlockSpec(memory_space=pltpu.VMEM)
    weights, places = pl.pallas_call(
        prep_kernel,
        out_shape=(
            jax.ShapeDtypeStruct((PLACES, TILE), jnp.float32),
            jax.ShapeDtypeStruct((PLACES,), jnp.int32),
        ),
        in_specs=[smem, vmem],
        out_specs=(vmem, smem),
    )(counts, gp_weights.reshape(-1, TILE))

    far0 = across_x(embeddings)
    near3 = across_z(embeddings, 3)
    near1 = across_z(embeddings, 1)
    half = enc_rows // 2
    head_mine = across_x(lax.dynamic_slice_in_dim(head_weight, rep * half, half, 0))
    head_other = across_cores(head_mine)
    far_head = jnp.where(
        rep == 0,
        jnp.concatenate([head_mine, head_other]),
        jnp.concatenate([head_other, head_mine]),
    )
    far0_next, weights, places = lax.optimization_barrier((far0, weights, places))
    near3, far_head = lax.optimization_barrier((near3, far_head))
    far2 = across_z(far0_next, 2)
    near2 = across_z(near3, 1)
    far1 = across_x(near1)
    far3 = across_x(near3)

    def features(near, far):
        value = jnp.dot(near, head_weight, preferred_element_type=jnp.float32)
        value += jnp.dot(far, far_head, preferred_element_type=jnp.float32)
        return value.astype(jnp.bfloat16)

    own0, own1 = features(embeddings, far0), features(near1, far1)
    other0, other1 = across_cores(own0), across_cores(own1)
    lent1 = across_cores(after(near1, own1))
    buffers = (
        jax.ShapeDtypeStruct((18 * TILE, width), jnp.bfloat16),
        jax.ShapeDtypeStruct((PLACES, TILE), jnp.float32),
        jax.ShapeDtypeStruct((12 * TILE, share_cols), jnp.bfloat16),
    )
    own2, own3 = features(near2, far2), features(near3, far3)
    other2, other3 = across_cores(own2), across_cores(own3)
    lent3 = across_cores(after(near3, own3))
    packed = pl.pallas_call(
        pack_kernel,
        out_shape=buffers,
        in_specs=[smem] + [vmem] * 11,
        out_specs=(vmem,) * 3,
        compiler_params=pltpu.CompilerParams(vmem_limit_bytes=30 * 2**20),
    )(
        places,
        embeddings,
        near1,
        near2,
        near3,
        lent1,
        own0,
        own1,
        own2,
        own3,
        other0,
        other1,
    )

    *_, own_grad, head_part, head_sent = pl.pallas_call(
        pair_kernel,
        out_shape=buffers
        + (
            jax.ShapeDtypeStruct((share_rows, width), jnp.bfloat16),
            jax.ShapeDtypeStruct((enc_rows, width), jnp.float32),
            jax.ShapeDtypeStruct((enc_rows, width), jnp.bfloat16),
        ),
        in_specs=[smem] + [vmem] * 7,
        out_specs=(vmem,) * 6,
        input_output_aliases={5: 0, 6: 1, 7: 2},
        scratch_shapes=[pltpu.VMEM((4 * CHUNK, width), jnp.bfloat16)],
        compiler_params=pltpu.CompilerParams(vmem_limit_bytes=40 * 2**20),
    )(places, weights, lent3, other2, other3, *packed)
    head_other_part = across_cores(head_sent)
    embed_grad = lax.dot_general(
        own_grad, head_weight, (((1,), (1,)), ((), ())), preferred_element_type=jnp.float32
    ).astype(jnp.bfloat16)
    head_grad = head_part + head_other_part.astype(jnp.float32)
    return embed_grad, head_grad


def solution(mesh):
    placed = (P(("groups", "loop", "rep"), "enc"), P("enc", None), P("groups"), P("groups"))
    sizes = dict(mesh.shape)

    def body(*arrays):
        share_rows = arrays[0].shape[0]
        small = sizes["loop"] == 4 and sizes["enc"] == 2 and sizes["rep"] == 2
        if small and share_rows == 2 * TILE:
            return gathered_body(*arrays)
        return ring_body(*arrays)

    return jax.shard_map(
        body,
        mesh=mesh,
        in_specs=placed,
        out_specs=(P(("groups", "loop", "rep"), "enc"), P(("groups", "enc"), None)),
        check_vma=False,
    )
```

```python
import jax
import jax.numpy as jnp
from jax import lax
from jax.experimental import pallas as pl
from jax.experimental.pallas import tpu as pltpu
from jax.sharding import PartitionSpec as P

EPSILON = 1e-06
TILE = 128
CHUNK = 2 * TILE


def passed_along(value, axis, steps):
    count = lax.axis_size(axis)
    pairs = [(source, (source + steps) % count) for source in range(count)]
    return lax.ppermute(value, axis, pairs)


def ring_body(embeddings, head_weight, gp_weights, counts):
    enc_size = lax.axis_size("enc")
    rep_size = lax.axis_size("rep")
    loop_size = lax.axis_size("loop")
    share_rows = embeddings.shape[0]
    piece_rows = share_rows // enc_size
    block_rows = share_rows * rep_size
    loop_index = lax.axis_index("loop")
    enc_index = lax.axis_index("enc")
    rep_index = lax.axis_index("rep")
    own_feats = lax.psum_scatter(
        jnp.dot(embeddings, head_weight, preferred_element_type=jnp.float32),
        "enc",
        scatter_dimension=0,
        tiled=True,
    ).astype(jnp.bfloat16)
    block_feats = lax.all_gather(own_feats, ("enc", "rep"), axis=0, tiled=True)
    block_norms = jnp.sum(jnp.square(block_feats.astype(jnp.float32)), axis=1)
    offsets = (
        jnp.arange(rep_size, dtype=jnp.int32)[None, :, None] * share_rows
        + jnp.arange(enc_size, dtype=jnp.int32)[:, None, None] * piece_rows
        + jnp.arange(piece_rows, dtype=jnp.int32)[None, None, :]
    ).reshape(block_rows)
    own_base = lax.dynamic_slice_in_dim(gp_weights, loop_index * block_rows, block_rows)
    block_coef = (
        own_base.reshape(rep_size, enc_size, piece_rows).transpose(1, 0, 2).reshape(block_rows)
    )
    own_count = lax.dynamic_index_in_dim(counts, loop_index, keepdims=False)
    block_coef = jnp.where(offsets < own_count, block_coef, 0.0)
    piece_start = rep_index * share_rows + enc_index * piece_rows
    piece_offsets = piece_start + jnp.arange(piece_rows, dtype=jnp.int32)

    def tile(state, piece, anchor):
        anchor_count = lax.dynamic_index_in_dim(counts, anchor, keepdims=False)
        accum, quotient_sum = state
        piece_coef = lax.dynamic_slice_in_dim(
            gp_weights, anchor * block_rows + piece_start, piece_rows
        )
        piece_coef = jnp.where(piece_offsets < anchor_count, piece_coef, 0.0)
        piece_norms = jnp.sum(jnp.square(piece.astype(jnp.float32)), axis=1)
        scores = lax.dot_general(
            piece, block_feats, (((1,), (1,)), ((), ())), preferred_element_type=jnp.float32
        )
        denom = piece_norms[:, None] + block_norms[None, :] - scores + EPSILON
        inverse = 1.0 / (denom * denom)
        pair_coef = piece_coef[:, None] * block_coef[None, :]
        pair_weight = (pair_coef * (piece_norms[:, None] + block_norms[None, :]) * inverse).astype(
            jnp.bfloat16
        )
        quotient_sum = quotient_sum + jnp.sum(pair_coef * 2.0 * scores * inverse, axis=0)
        accum = accum + lax.dot_general(
            pair_weight, piece, (((0,), (0,)), ((), ())), preferred_element_type=jnp.float32
        )
        return (accum, quotient_sum)

    start_state = (
        jnp.zeros((block_rows, block_feats.shape[1]), jnp.float32),
        jnp.zeros((block_rows,), jnp.float32),
    )
    state = tile(start_state, own_feats, loop_index)

    def forward_step(step_index, carry):
        moving, inner = carry
        moving = passed_along(moving, "loop", 1)
        inner = tile(inner, moving, (loop_index - step_index - 1 + loop_size) % loop_size)
        return (moving, inner)

    moving, state = lax.fori_loop(0, loop_size - 1, forward_step, (own_feats, state))
    accum, quotient_sum = state
    grad_block = accum - block_feats.astype(jnp.float32) * quotient_sum[:, None]
    own_grad = lax.psum_scatter(
        grad_block.astype(jnp.bfloat16), ("enc", "rep"), scatter_dimension=0, tiled=True
    )
    piece = lax.all_gather(own_grad, "enc", axis=0, tiled=True)
    embed_part = lax.dot_general(
        piece, head_weight, (((1,), (1,)), ((), ())), preferred_element_type=jnp.float32
    )
    head_part = lax.dot_general(
        embeddings, piece, (((0,), (0,)), ((), ())), preferred_element_type=jnp.float32
    )
    head_grad = lax.psum(head_part, ("loop", "rep"))
    return (embed_part.astype(jnp.bfloat16), head_grad)


OWN_ORDER = ((0, 0), (0, 1), (2, 0), (2, 1), (3, 1), (3, 0), (1, 1), (1, 0))
SLOTS = [(0, k, h) for k, h in OWN_ORDER] + [(1, k, h) for k, h in OWN_ORDER[::-1]]
LENT = ((1, 0), (1, 1), (3, 0), (3, 1))
PLACES = 24


def turned(row):
    return jnp.transpose(jnp.broadcast_to(row, (TILE, TILE)))[:, :1]


def prep_kernel(counts_ref, gp_ref, weights, places):
    z = lax.axis_index("loop")
    rep = lax.axis_index("rep")
    lane = lax.broadcasted_iota(jnp.int32, (1, TILE), 1)
    weights[...] = jnp.zeros_like(weights)
    total = jnp.int32(0)
    totals = []
    for slot, (other, k, h) in enumerate(SLOTS):
        block = jnp.bitwise_xor(z, k)
        piece = rep if other == 0 else 1 - rep
        base = piece * (2 * TILE) + h * TILE
        count = counts_ref[block]
        valid = count > base

        @pl.when(valid)
        def _(block=block, piece=piece, h=h, base=base, count=count, total=total):
            row = gp_ref[pl.ds(block * 4 + piece * 2 + h, 1), :]
            weights[pl.ds(total, 1), :] = jnp.where(lane + base < count, row, 0.0)

        places[slot] = jnp.where(valid, total, -1)
        total = total + valid.astype(jnp.int32)
        totals.append(total)
    own = totals[len(OWN_ORDER) - 1]
    places[16] = total
    places[17] = jnp.where(rep == 0, (total + 1) // 2, total // 2)
    places[18] = jnp.clip(counts_ref[z] - rep * (2 * TILE), 0, 2 * TILE)
    places[19] = own


def tile_at(place):
    return pl.ds(pl.multiple_of(place * TILE, TILE), TILE)


def pack_tiles(places, pieces, rows_of, feats, norms, near):
    width = feats.shape[1]
    for slot, (other, k, h) in enumerate(SLOTS):
        if (other, k) not in pieces:
            continue
        place = places[slot]

        @pl.when(place >= 0)
        def _(place=place, other=other, k=k, h=h):
            here = slice(h * TILE, (h + 1) * TILE)
            value = pieces[other, k][here, :]
            feats[tile_at(place), :] = value
            wide = value.astype(jnp.float32)
            square = wide * wide
            part = square[:, :TILE]
            for s in range(1, width // TILE):
                part += square[:, s * TILE : (s + 1) * TILE]
            norms[pl.ds(place, 1), :] = jnp.sum(jnp.transpose(part), axis=0, keepdims=True)
            if (other, k) in rows_of:
                near[tile_at(place), :] = rows_of[other, k][here, :]


def pack_kernel(
    places,
    near0,
    near1,
    near2,
    near3,
    lent1,
    own0,
    own1,
    own2,
    own3,
    other0,
    other1,
    feats,
    norms,
    near,
):
    pieces = {
        (0, 0): own0,
        (0, 1): own1,
        (0, 2): own2,
        (0, 3): own3,
        (1, 0): other0,
        (1, 1): other1,
    }
    rows_of = {(0, 0): near0, (0, 1): near1, (0, 2): near2, (0, 3): near3, (1, 1): lent1}
    pack_tiles(places, pieces, rows_of, feats, norms, near)


def pair_kernel(
    places,
    weights,
    lent3,
    other2,
    other3,
    feats_in,
    norms_in,
    near_in,
    feats,
    norms,
    near,
    own_out,
    head_sent,
    grads,
):
    del feats_in, norms_in, near_in
    width = feats.shape[1]
    total, rows_here, own_valid = places[16], places[17], places[18]
    pack_tiles(
        places, {(1, 2): other2, (1, 3): other3}, {(1, 3): lent3}, feats, norms, near
    )
    feats[tile_at(total), :] = jnp.zeros((TILE, width), jnp.bfloat16)
    norms[pl.ds(total, 1), :] = jnp.zeros((1, TILE), jnp.float32)

    def row_chunk(i, deep, tiles):
        size = deep * TILE
        rows = pl.ds(pl.multiple_of(i * size, TILE), size)
        left = feats[rows, :]
        right = feats[: tiles * TILE, :]
        places_of = [pl.ds(deep * i + t, 1) for t in range(deep)]
        left_norms = jnp.concatenate([turned(norms[at, :]) for at in places_of], axis=0)
        coef = jnp.concatenate([turned(weights[at, :]) for at in places_of], axis=0)
        scores = lax.dot_general(
            left, right, (((1,), (1,)), ((), ())), preferred_element_type=jnp.float32
        )
        all_norms = jnp.concatenate([norms[t : t + 1, :] for t in range(tiles)], axis=1)
        all_coef = jnp.concatenate([weights[t : t + 1, :] for t in range(tiles)], axis=1)
        both = left_norms + all_norms
        denom = both - scores + EPSILON
        scaled = all_coef * (1.0 / (denom * denom))
        pair = (scaled * both).astype(jnp.bfloat16)
        quotient = 2.0 * jnp.sum(scaled * scores, axis=1, keepdims=True)
        carried = jnp.dot(pair, right, preferred_element_type=jnp.float32)
        row = lax.broadcasted_iota(jnp.int32, (size, 1), 0) + i * size
        coef = jnp.where(row < rows_here * TILE, coef, 0.0)
        grad = coef * (carried - left.astype(jnp.float32) * quotient)
        grads[rows, :] = grad.astype(jnp.bfloat16)

    row_tiles = jnp.maximum(2 * ((rows_here + 1) // 2), 4)

    @pl.when(row_tiles > rows_here)
    def _():
        near[tile_at(row_tiles - 1), :] = jnp.zeros((TILE, near.shape[1]), near.dtype)

    col_tiles = jnp.maximum(2 * ((total + 1) // 2), 8)
    for count, deep, columns in ((4, 2, (8, 10)), (6, 3, (10, 12, 14)), (8, 2, (14,))):
        for tiles in columns:

            @pl.when(jnp.logical_and(col_tiles == tiles, row_tiles == count))
            def _(count=count, deep=deep, tiles=tiles):
                def step(i, _):
                    row_chunk(i, deep, tiles)
                    return 0

                lax.fori_loop(0, count // deep, step, 0)

        @pl.when(row_tiles == count)
        def _(count=count):
            rows = slice(0, count * TILE)
            head = lax.dot_general(
                near[rows, :],
                grads[rows, :],
                (((0,), (0,)), ((), ())),
                preferred_element_type=jnp.float32,
            )
            head_sent[...] = head.astype(jnp.bfloat16)

    own = grads[:CHUNK, :]
    row = lax.broadcasted_iota(jnp.int32, (CHUNK, 1), 0)
    own_out[...] = jnp.where(row < own_valid, own, jnp.zeros_like(own))


def gathered_body(embeddings, head_weight, gp_weights, counts):
    loop_size = lax.axis_size("loop")
    rep = lax.axis_index("rep")
    share_rows, share_cols = embeddings.shape
    enc_rows, width = head_weight.shape

    def across_z(value, step):
        return lax.ppermute(value, "loop", [(i, i ^ step) for i in range(loop_size)])

    def across_x(value):
        return lax.ppermute(value, "enc", [(0, 1), (1, 0)])

    def across_cores(value):
        return lax.ppermute(value, "rep", [(0, 1), (1, 0)])

    def after(value, *others):
        return lax.optimization_barrier((value, *others))[0]

    smem = pl.BlockSpec(memory_space=pltpu.SMEM)
    vmem = pl.BlockSpec(memory_space=pltpu.VMEM)
    weights, places = pl.pallas_call(
        prep_kernel,
        out_shape=(
            jax.ShapeDtypeStruct((PLACES, TILE), jnp.float32),
            jax.ShapeDtypeStruct((PLACES,), jnp.int32),
        ),
        in_specs=[smem, vmem],
        out_specs=(vmem, smem),
    )(counts, gp_weights.reshape(-1, TILE))

    far0 = across_x(embeddings)
    near3 = across_z(embeddings, 3)
    near1 = across_z(embeddings, 1)
    half = enc_rows // 2
    head_mine = across_x(lax.dynamic_slice_in_dim(head_weight, rep * half, half, 0))
    head_other = across_cores(head_mine)
    far_head = jnp.where(
        rep == 0,
        jnp.concatenate([head_mine, head_other]),
        jnp.concatenate([head_other, head_mine]),
    )
    far0_next, weights, places = lax.optimization_barrier((far0, weights, places))
    near3, far_head = lax.optimization_barrier((near3, far_head))
    far2 = across_z(far0_next, 2)
    near2 = across_z(near3, 1)
    far1 = across_x(near1)
    far3 = across_x(near3)

    def features(near, far):
        value = jnp.dot(near, head_weight, preferred_element_type=jnp.float32)
        value += jnp.dot(far, far_head, preferred_element_type=jnp.float32)
        return value.astype(jnp.bfloat16)

    own0, own1 = features(embeddings, far0), features(near1, far1)
    other0, other1 = across_cores(own0), across_cores(own1)
    lent1 = across_cores(after(near1, own1))
    buffers = (
        jax.ShapeDtypeStruct((18 * TILE, width), jnp.bfloat16),
        jax.ShapeDtypeStruct((PLACES, TILE), jnp.float32),
        jax.ShapeDtypeStruct((12 * TILE, share_cols), jnp.bfloat16),
    )
    own2, own3 = features(near2, far2), features(near3, far3)
    other2, other3 = across_cores(own2), across_cores(own3)
    lent3 = across_cores(after(near3, own3))
    packed = pl.pallas_call(
        pack_kernel,
        out_shape=buffers,
        in_specs=[smem] + [vmem] * 11,
        out_specs=(vmem,) * 3,
        compiler_params=pltpu.CompilerParams(vmem_limit_bytes=30 * 2**20),
    )(
        places,
        embeddings,
        near1,
        near2,
        near3,
        lent1,
        own0,
        own1,
        own2,
        own3,
        other0,
        other1,
    )

    *_, own_grad, head_sent = pl.pallas_call(
        pair_kernel,
        out_shape=buffers
        + (
            jax.ShapeDtypeStruct((share_rows, width), jnp.bfloat16),
            jax.ShapeDtypeStruct((enc_rows, width), jnp.bfloat16),
        ),
        in_specs=[smem] + [vmem] * 7,
        out_specs=(vmem,) * 5,
        input_output_aliases={5: 0, 6: 1, 7: 2},
        scratch_shapes=[pltpu.VMEM((4 * CHUNK, width), jnp.bfloat16)],
        compiler_params=pltpu.CompilerParams(vmem_limit_bytes=40 * 2**20),
    )(places, weights, lent3, other2, other3, *packed)
    head_other_part = across_cores(head_sent)
    embed_grad = lax.dot_general(
        own_grad, head_weight, (((1,), (1,)), ((), ())), preferred_element_type=jnp.float32
    ).astype(jnp.bfloat16)
    head_grad = head_sent.astype(jnp.float32) + head_other_part.astype(jnp.float32)
    return embed_grad, head_grad


def solution(mesh):
    placed = (P(("groups", "loop", "rep"), "enc"), P("enc", None), P("groups"), P("groups"))
    sizes = dict(mesh.shape)

    def body(*arrays):
        share_rows = arrays[0].shape[0]
        small = sizes["loop"] == 4 and sizes["enc"] == 2 and sizes["rep"] == 2
        if small and share_rows == 2 * TILE:
            return gathered_body(*arrays)
        return ring_body(*arrays)

    return jax.shard_map(
        body,
        mesh=mesh,
        in_specs=placed,
        out_specs=(P(("groups", "loop", "rep"), "enc"), P(("groups", "enc"), None)),
        check_vma=False,
    )
```

```python
import jax
import jax.numpy as jnp
from jax import lax
from jax.experimental import pallas as pl
from jax.experimental.pallas import tpu as pltpu
from jax.sharding import PartitionSpec as P

EPSILON = 1e-06
TILE = 128
CHUNK = 2 * TILE


def passed_along(value, axis, steps):
    count = lax.axis_size(axis)
    pairs = [(source, (source + steps) % count) for source in range(count)]
    return lax.ppermute(value, axis, pairs)


def ring_body(embeddings, head_weight, gp_weights, counts):
    enc_size = lax.axis_size("enc")
    rep_size = lax.axis_size("rep")
    loop_size = lax.axis_size("loop")
    share_rows = embeddings.shape[0]
    piece_rows = share_rows // enc_size
    block_rows = share_rows * rep_size
    loop_index = lax.axis_index("loop")
    enc_index = lax.axis_index("enc")
    rep_index = lax.axis_index("rep")
    own_feats = lax.psum_scatter(
        jnp.dot(embeddings, head_weight, preferred_element_type=jnp.float32),
        "enc",
        scatter_dimension=0,
        tiled=True,
    ).astype(jnp.bfloat16)
    block_feats = lax.all_gather(own_feats, ("enc", "rep"), axis=0, tiled=True)
    block_norms = jnp.sum(jnp.square(block_feats.astype(jnp.float32)), axis=1)
    offsets = (
        jnp.arange(rep_size, dtype=jnp.int32)[None, :, None] * share_rows
        + jnp.arange(enc_size, dtype=jnp.int32)[:, None, None] * piece_rows
        + jnp.arange(piece_rows, dtype=jnp.int32)[None, None, :]
    ).reshape(block_rows)
    own_base = lax.dynamic_slice_in_dim(gp_weights, loop_index * block_rows, block_rows)
    block_coef = (
        own_base.reshape(rep_size, enc_size, piece_rows).transpose(1, 0, 2).reshape(block_rows)
    )
    own_count = lax.dynamic_index_in_dim(counts, loop_index, keepdims=False)
    block_coef = jnp.where(offsets < own_count, block_coef, 0.0)
    piece_start = rep_index * share_rows + enc_index * piece_rows
    piece_offsets = piece_start + jnp.arange(piece_rows, dtype=jnp.int32)

    def tile(state, piece, anchor):
        anchor_count = lax.dynamic_index_in_dim(counts, anchor, keepdims=False)
        accum, quotient_sum = state
        piece_coef = lax.dynamic_slice_in_dim(
            gp_weights, anchor * block_rows + piece_start, piece_rows
        )
        piece_coef = jnp.where(piece_offsets < anchor_count, piece_coef, 0.0)
        piece_norms = jnp.sum(jnp.square(piece.astype(jnp.float32)), axis=1)
        scores = lax.dot_general(
            piece, block_feats, (((1,), (1,)), ((), ())), preferred_element_type=jnp.float32
        )
        denom = piece_norms[:, None] + block_norms[None, :] - scores + EPSILON
        inverse = 1.0 / (denom * denom)
        pair_coef = piece_coef[:, None] * block_coef[None, :]
        pair_weight = (pair_coef * (piece_norms[:, None] + block_norms[None, :]) * inverse).astype(
            jnp.bfloat16
        )
        quotient_sum = quotient_sum + jnp.sum(pair_coef * 2.0 * scores * inverse, axis=0)
        accum = accum + lax.dot_general(
            pair_weight, piece, (((0,), (0,)), ((), ())), preferred_element_type=jnp.float32
        )
        return (accum, quotient_sum)

    start_state = (
        jnp.zeros((block_rows, block_feats.shape[1]), jnp.float32),
        jnp.zeros((block_rows,), jnp.float32),
    )
    state = tile(start_state, own_feats, loop_index)

    def forward_step(step_index, carry):
        moving, inner = carry
        moving = passed_along(moving, "loop", 1)
        inner = tile(inner, moving, (loop_index - step_index - 1 + loop_size) % loop_size)
        return (moving, inner)

    moving, state = lax.fori_loop(0, loop_size - 1, forward_step, (own_feats, state))
    accum, quotient_sum = state
    grad_block = accum - block_feats.astype(jnp.float32) * quotient_sum[:, None]
    own_grad = lax.psum_scatter(
        grad_block.astype(jnp.bfloat16), ("enc", "rep"), scatter_dimension=0, tiled=True
    )
    piece = lax.all_gather(own_grad, "enc", axis=0, tiled=True)
    embed_part = lax.dot_general(
        piece, head_weight, (((1,), (1,)), ((), ())), preferred_element_type=jnp.float32
    )
    head_part = lax.dot_general(
        embeddings, piece, (((0,), (0,)), ((), ())), preferred_element_type=jnp.float32
    )
    head_grad = lax.psum(head_part, ("loop", "rep"))
    return (embed_part.astype(jnp.bfloat16), head_grad)


OWN_ORDER = ((0, 0), (0, 1), (2, 0), (2, 1), (3, 1), (3, 0), (1, 1), (1, 0))
SLOTS = [(0, k, h) for k, h in OWN_ORDER] + [(1, k, h) for k, h in OWN_ORDER[::-1]]
LENT = ((1, 0), (1, 1), (3, 0), (3, 1))
PLACES = 24


def turned(row):
    return jnp.transpose(jnp.broadcast_to(row, (TILE, TILE)))[:, :1]


def prep_kernel(counts_ref, gp_ref, weights, places):
    z = lax.axis_index("loop")
    rep = lax.axis_index("rep")
    lane = lax.broadcasted_iota(jnp.int32, (1, TILE), 1)
    weights[...] = jnp.zeros_like(weights)
    total = jnp.int32(0)
    totals = []
    for slot, (other, k, h) in enumerate(SLOTS):
        block = jnp.bitwise_xor(z, k)
        piece = rep if other == 0 else 1 - rep
        base = piece * (2 * TILE) + h * TILE
        count = counts_ref[block]
        valid = count > base

        @pl.when(valid)
        def _(block=block, piece=piece, h=h, base=base, count=count, total=total):
            row = gp_ref[pl.ds(block * 4 + piece * 2 + h, 1), :]
            weights[pl.ds(total, 1), :] = jnp.where(lane + base < count, row, 0.0)

        places[slot] = jnp.where(valid, total, -1)
        total = total + valid.astype(jnp.int32)
        totals.append(total)
    own = totals[len(OWN_ORDER) - 1]
    places[16] = total
    places[17] = jnp.where(rep == 0, (total + 1) // 2, total // 2)
    places[18] = jnp.clip(counts_ref[z] - rep * (2 * TILE), 0, 2 * TILE)
    places[19] = own


def tile_at(place):
    return pl.ds(pl.multiple_of(place * TILE, TILE), TILE)


def pack_tiles(places, pieces, rows_of, feats, norms, near):
    width = feats.shape[1]
    for slot, (other, k, h) in enumerate(SLOTS):
        if (other, k) not in pieces:
            continue
        place = places[slot]

        @pl.when(place >= 0)
        def _(place=place, other=other, k=k, h=h):
            here = slice(h * TILE, (h + 1) * TILE)
            value = pieces[other, k][here, :]
            feats[tile_at(place), :] = value
            wide = value.astype(jnp.float32)
            square = wide * wide
            part = square[:, :TILE]
            for s in range(1, width // TILE):
                part += square[:, s * TILE : (s + 1) * TILE]
            norms[pl.ds(place, 1), :] = jnp.sum(jnp.transpose(part), axis=0, keepdims=True)
            if (other, k) in rows_of:
                near[tile_at(place), :] = rows_of[other, k][here, :]


def pack_kernel(
    places,
    near0,
    near1,
    near2,
    near3,
    lent1,
    own0,
    own1,
    own2,
    own3,
    other0,
    other1,
    feats,
    norms,
    near,
):
    pieces = {
        (0, 0): own0,
        (0, 1): own1,
        (0, 2): own2,
        (0, 3): own3,
        (1, 0): other0,
        (1, 1): other1,
    }
    rows_of = {(0, 0): near0, (0, 1): near1, (0, 2): near2, (0, 3): near3, (1, 1): lent1}
    pack_tiles(places, pieces, rows_of, feats, norms, near)


def pair_kernel(
    places,
    weights,
    lent3,
    other2,
    other3,
    feats_in,
    norms_in,
    near_in,
    feats,
    norms,
    near,
    own_out,
    head_out,
    head_sent,
    grads,
):
    del feats_in, norms_in, near_in
    width = feats.shape[1]
    total, rows_here, own_valid = places[16], places[17], places[18]
    pack_tiles(
        places, {(1, 2): other2, (1, 3): other3}, {(1, 3): lent3}, feats, norms, near
    )
    feats[tile_at(total), :] = jnp.zeros((TILE, width), jnp.bfloat16)
    norms[pl.ds(total, 1), :] = jnp.zeros((1, TILE), jnp.float32)

    def row_chunk(i, deep, tiles):
        size = deep * TILE
        rows = pl.ds(pl.multiple_of(i * size, TILE), size)
        left = feats[rows, :]
        right = feats[: tiles * TILE, :]
        places_of = [pl.ds(deep * i + t, 1) for t in range(deep)]
        left_norms = jnp.concatenate([turned(norms[at, :]) for at in places_of], axis=0)
        coef = jnp.concatenate([turned(weights[at, :]) for at in places_of], axis=0)
        scores = lax.dot_general(
            left, right, (((1,), (1,)), ((), ())), preferred_element_type=jnp.float32
        )
        all_norms = jnp.concatenate([norms[t : t + 1, :] for t in range(tiles)], axis=1)
        all_coef = jnp.concatenate([weights[t : t + 1, :] for t in range(tiles)], axis=1)
        both = left_norms + all_norms
        denom = both - scores + EPSILON
        scaled = all_coef * (1.0 / (denom * denom))
        pair = (scaled * both).astype(jnp.bfloat16)
        quotient = 2.0 * jnp.sum(scaled * scores, axis=1, keepdims=True)
        carried = jnp.dot(pair, right, preferred_element_type=jnp.float32)
        row = lax.broadcasted_iota(jnp.int32, (size, 1), 0) + i * size
        coef = jnp.where(row < rows_here * TILE, coef, 0.0)
        grad = coef * (carried - left.astype(jnp.float32) * quotient)
        grads[rows, :] = grad.astype(jnp.bfloat16)

    row_tiles = jnp.maximum(2 * ((rows_here + 1) // 2), 4)

    @pl.when(row_tiles > rows_here)
    def _():
        near[tile_at(row_tiles - 1), :] = jnp.zeros((TILE, near.shape[1]), near.dtype)

    col_tiles = jnp.maximum(2 * ((total + 1) // 2), 8)
    for count, deep, columns in ((4, 4, (8, 10)), (6, 3, (10, 12, 14)), (8, 4, (14,))):
        for tiles in columns:

            @pl.when(jnp.logical_and(col_tiles == tiles, row_tiles == count))
            def _(count=count, deep=deep, tiles=tiles):
                def step(i, _):
                    row_chunk(i, deep, tiles)
                    return 0

                lax.fori_loop(0, count // deep, step, 0)

        @pl.when(row_tiles == count)
        def _(count=count):
            rows = slice(0, count * TILE)
            head = lax.dot_general(
                near[rows, :],
                grads[rows, :],
                (((0,), (0,)), ((), ())),
                preferred_element_type=jnp.float32,
            )
            head_out[...] = head
            head_sent[...] = head.astype(jnp.bfloat16)

    own = grads[:CHUNK, :]
    row = lax.broadcasted_iota(jnp.int32, (CHUNK, 1), 0)
    own_out[...] = jnp.where(row < own_valid, own, jnp.zeros_like(own))


def gathered_body(embeddings, head_weight, gp_weights, counts):
    loop_size = lax.axis_size("loop")
    rep = lax.axis_index("rep")
    share_rows, share_cols = embeddings.shape
    enc_rows, width = head_weight.shape

    def across_z(value, step):
        return lax.ppermute(value, "loop", [(i, i ^ step) for i in range(loop_size)])

    def across_x(value):
        return lax.ppermute(value, "enc", [(0, 1), (1, 0)])

    def across_cores(value):
        return lax.ppermute(value, "rep", [(0, 1), (1, 0)])

    def after(value, *others):
        return lax.optimization_barrier((value, *others))[0]

    smem = pl.BlockSpec(memory_space=pltpu.SMEM)
    vmem = pl.BlockSpec(memory_space=pltpu.VMEM)
    weights, places = pl.pallas_call(
        prep_kernel,
        out_shape=(
            jax.ShapeDtypeStruct((PLACES, TILE), jnp.float32),
            jax.ShapeDtypeStruct((PLACES,), jnp.int32),
        ),
        in_specs=[smem, vmem],
        out_specs=(vmem, smem),
    )(counts, gp_weights.reshape(-1, TILE))

    far0 = across_x(embeddings)
    near3 = across_z(embeddings, 3)
    near1 = across_z(embeddings, 1)
    half = enc_rows // 2
    head_mine = across_x(lax.dynamic_slice_in_dim(head_weight, rep * half, half, 0))
    head_other = across_cores(head_mine)
    far_head = jnp.where(
        rep == 0,
        jnp.concatenate([head_mine, head_other]),
        jnp.concatenate([head_other, head_mine]),
    )
    far0_next, weights, places = lax.optimization_barrier((far0, weights, places))
    near3, far_head = lax.optimization_barrier((near3, far_head))
    far2 = across_z(far0_next, 2)
    near2 = across_z(near3, 1)
    far1 = across_x(near1)
    far3 = across_x(near3)

    def features(near, far):
        value = jnp.dot(near, head_weight, preferred_element_type=jnp.float32)
        value += jnp.dot(far, far_head, preferred_element_type=jnp.float32)
        return value.astype(jnp.bfloat16)

    own0, own1 = features(embeddings, far0), features(near1, far1)
    other0, other1 = across_cores(own0), across_cores(own1)
    lent1 = across_cores(after(near1, own1))
    buffers = (
        jax.ShapeDtypeStruct((18 * TILE, width), jnp.bfloat16),
        jax.ShapeDtypeStruct((PLACES, TILE), jnp.float32),
        jax.ShapeDtypeStruct((12 * TILE, share_cols), jnp.bfloat16),
    )
    own2, own3 = features(near2, far2), features(near3, far3)
    other2, other3 = across_cores(own2), across_cores(own3)
    lent3 = across_cores(after(near3, own3))
    packed = pl.pallas_call(
        pack_kernel,
        out_shape=buffers,
        in_specs=[smem] + [vmem] * 11,
        out_specs=(vmem,) * 3,
        compiler_params=pltpu.CompilerParams(vmem_limit_bytes=30 * 2**20),
    )(
        places,
        embeddings,
        near1,
        near2,
        near3,
        lent1,
        own0,
        own1,
        own2,
        own3,
        other0,
        other1,
    )

    *_, own_grad, head_part, head_sent = pl.pallas_call(
        pair_kernel,
        out_shape=buffers
        + (
            jax.ShapeDtypeStruct((share_rows, width), jnp.bfloat16),
            jax.ShapeDtypeStruct((enc_rows, width), jnp.float32),
            jax.ShapeDtypeStruct((enc_rows, width), jnp.bfloat16),
        ),
        in_specs=[smem] + [vmem] * 7,
        out_specs=(vmem,) * 6,
        input_output_aliases={5: 0, 6: 1, 7: 2},
        scratch_shapes=[pltpu.VMEM((4 * CHUNK, width), jnp.bfloat16)],
        compiler_params=pltpu.CompilerParams(vmem_limit_bytes=40 * 2**20),
    )(places, weights, lent3, other2, other3, *packed)
    head_other_part = across_cores(head_sent)
    embed_grad = lax.dot_general(
        own_grad, head_weight, (((1,), (1,)), ((), ())), preferred_element_type=jnp.float32
    ).astype(jnp.bfloat16)
    head_grad = head_part + head_other_part.astype(jnp.float32)
    return embed_grad, head_grad


def solution(mesh):
    placed = (P(("groups", "loop", "rep"), "enc"), P("enc", None), P("groups"), P("groups"))
    sizes = dict(mesh.shape)

    def body(*arrays):
        share_rows = arrays[0].shape[0]
        small = sizes["loop"] == 4 and sizes["enc"] == 2 and sizes["rep"] == 2
        if small and share_rows == 2 * TILE:
            return gathered_body(*arrays)
        return ring_body(*arrays)

    return jax.shard_map(
        body,
        mesh=mesh,
        in_specs=placed,
        out_specs=(P(("groups", "loop", "rep"), "enc"), P(("groups", "enc"), None)),
        check_vma=False,
    )
```
